512 devices in a mesh: seq: 16 (over z, core), exp: 32 (over y, x).
Axes of the slice: x: 4, y: 8, z: 8, core: 2. Of those that a mesh axis runs over, the one named last changes fastest.
Arguments:
- query_rows: bfloat16 [32768, 1024], P(('exp', 'seq')), may hold values from -8 to 8
- key_rows: bfloat16 [32768, 1024], P(('exp', 'seq')), may hold values from -8 to 8
- value_rows: bfloat16 [32768, 1024], P(('exp', 'seq')), may hold values from -6 to 6
- query_tangent: bfloat16 [32768, 1024], P(('exp', 'seq')), may hold values from -6 to 6
- key_tangent: bfloat16 [32768, 1024], P(('exp', 'seq')), may hold values from -6 to 6
- value_tangent: bfloat16 [32768, 1024], P(('exp', 'seq')), may hold values from -6 to 6
- stream: bfloat16 [32768, 1024], P(('exp', 'seq')), may hold values from -16 to 16
- stream_tangent: bfloat16 [32768, 1024], P(('exp', 'seq')), may hold values from -6 to 6
- norm_gain: float32 [1024], replicated, may hold values from 0.1 to 1.9
- expert_ids: int32 [32768, 2], P(('exp', 'seq')), may hold values from 0 to 15, as said below
- gate_units: int32 [32768, 2], P(('exp', 'seq')), may hold values from 4096 to 61440, as said below
- slot_index: int32 [32768, 2], P(('exp', 'seq')), may hold values from -1 to 9, as said below
- weight_in: bfloat16 [1024, 65536], P(None, ('exp', 'seq')), may hold values from -0.1875 to 0.1875
- weight_out: bfloat16 [65536, 1024], P(('exp', 'seq')), may hold values from -0.09375 to 0.09375
Outputs:
- block_out: bfloat16 [32768, 1024], P(('exp', 'seq'))
- block_tangent: bfloat16 [32768, 1024], P(('exp', 'seq'))
The draws below stay inside these ranges and needn't reach their ends.
Inputs may be any that keep to these rules, and one draw needn't show every extreme that they name: `expert_ids`: each token names two different experts. In every aligned block of 64 rows one expert is named by more than 10 tokens. `gate_units`: the two gates of a token sum to 65536; the first is the larger or equal one. `slot_index`: within an aligned block of 64 rows the kept assignments to one expert hold the slots 0, 1, 2 and so on, each once, in no particular order; assignments beyond 10 are -1. Every block fills all 10 slots of some expert.
All inputs are finite; a program needn't handle non-finite values.
Results may differ from the reference program's by a relative error of at most 0.0059.
Values may be sent and summed in bfloat16 or wider, within the bound.
A program may use at most 64 MiB of HBM per device.

```python
import math
import jax
import jax.numpy as jnp
from jax import lax

D = 1024
HEADS = 16
HEAD_DIM = 64
FF = 4096
TOK_DEV = 64
GROUP = 1024
TOKENS = 32768
EXPERTS = 16
CAP = 10
SLICE = 2048
N_EXP = 32


def draw_query_rows(key, part):
    key = jax.random.fold_in(key, 1)
    base = jnp.clip(jax.random.normal(key, (TOKENS, D), jnp.float32), -6.0, 6.0)
    return base.astype(jnp.bfloat16)


def draw_key_rows(key, part):
    key = jax.random.fold_in(key, 2)
    base = jnp.clip(jax.random.normal(key, (TOKENS, D), jnp.float32), -6.0, 6.0)
    return base.astype(jnp.bfloat16)


def draw_stream(key, part):
    key = jax.random.fold_in(key, 3)
    base_key, row_key, column_key = jax.random.split(key, 3)
    base = jnp.clip(jax.random.normal(base_key, (TOKENS, D), jnp.float32), -4.0, 4.0)
    row_scales = jnp.exp(jax.random.uniform(row_key, (TOKENS, 1), jnp.float32, math.log(0.25), math.log(2.5)))
    column_scales = jnp.exp(jax.random.uniform(column_key, (1, D), jnp.float32, math.log(0.4), math.log(1.6)))
    return (base * row_scales * column_scales).astype(jnp.bfloat16)


def routing(key):
    key = jax.random.fold_in(key, 202)
    first_key, offset_key, busy_key, rank_key, order_key = jax.random.split(key, 5)
    block_count = TOKENS // TOK_DEV
    seq_count = GROUP // TOK_DEV
    first_pick = jax.random.randint(first_key, (block_count, TOK_DEV), 0, EXPERTS)
    offsets = jax.random.randint(offset_key, (block_count, TOK_DEV), 1, EXPERTS)
    busy_table = jax.random.randint(busy_key, (seq_count,), 0, EXPERTS)
    block_numbers = lax.broadcasted_iota(jnp.int32, (block_count, 1), 0)
    busiest = busy_table[block_numbers % seq_count]
    position = lax.broadcasted_iota(jnp.int32, (block_count, TOK_DEV), 1)
    scored = jax.random.randint(rank_key, (block_count, TOK_DEV), 0, 1 << 20) * TOK_DEV + position
    ranking = jnp.argsort(jnp.argsort(scored, axis=1), axis=1)
    first_pick = jnp.where(ranking <= CAP, busiest, first_pick)
    second_pick = (first_pick + offsets) % EXPERTS
    chosen = jnp.stack((first_pick, second_pick), axis=-1).reshape(block_count, 2 * TOK_DEV)
    lanes = lax.broadcasted_iota(jnp.int32, (block_count, 2 * TOK_DEV), 1)
    priority = jax.random.randint(order_key, (block_count, 2 * TOK_DEV), 0, 1 << 20) * (2 * TOK_DEV) + lanes
    same_expert = chosen[:, :, None] == chosen[:, None, :]
    earlier = priority[:, None, :] < priority[:, :, None]
    counted = jnp.sum((same_expert & earlier).astype(jnp.int32), axis=2)
    slots = jnp.where(counted < CAP, counted, -1)
    return (chosen.reshape(TOKENS, 2).astype(jnp.int32), slots.reshape(TOKENS, 2).astype(jnp.int32))


def draw_expert_ids(key, part):
    return routing(key)[0]


def draw_slot_index(key, part):
    return routing(key)[1]


def draw_gate_units(key, part):
    key = jax.random.fold_in(key, 7)
    larger = jax.random.randint(key, (TOKENS, 1), 32768, 61441)
    return jnp.concatenate((larger, 65536 - larger), axis=1).astype(jnp.int32)


def level_of(rng, dims, cuts, least, top_value):
    loudness, own = 1.0, jax.random.fold_in(rng, 6)
    for dim, blocks in cuts:
        steps = jnp.exp(jax.random.uniform(jax.random.fold_in(own, dim), (blocks,), jnp.float32, least / len(cuts), top_value / len(cuts)))
        loudness = loudness * jnp.repeat(steps, dims[dim] // blocks).reshape([-1 if axis == dim else 1 for axis in range(len(dims))])
    return loudness


def normal_values(key, dims, scale, reach, cuts=(), kind=jnp.bfloat16):
    factor_of = level_of(key, dims, cuts, -0.22, 0.18) if cuts else 1.0
    drawn = jax.random.normal(key, dims, jnp.float32) * scale * factor_of
    return jnp.minimum(jnp.maximum(drawn, -reach), reach).astype(kind)


def setup_inputs(seed: int = 0) -> dict:
    key_of = jax.random.split(jax.random.key(seed), 15)
    query_rows = draw_query_rows(jax.random.fold_in(key_of[14], 71), 0)
    key_rows = draw_key_rows(jax.random.fold_in(key_of[14], 71), 0)
    value_rows = normal_values(key_of[2], (TOKENS, D), 1.0, 6.0, ((0, 512),))
    query_tangent = normal_values(key_of[3], (TOKENS, D), 1.0, 6.0, ((0, 512),))
    key_tangent = normal_values(key_of[4], (TOKENS, D), 1.0, 6.0, ((0, 512),))
    value_tangent = normal_values(key_of[5], (TOKENS, D), 1.0, 6.0, ((0, 512),))
    stream = draw_stream(jax.random.fold_in(key_of[14], 71), 0)
    stream_tangent = normal_values(key_of[7], (TOKENS, D), 1.0, 6.0, ((0, 512),))
    norm_gain = jnp.clip(1.0 + 0.18 * jax.random.normal(key_of[8], (D,), jnp.float32), 0.1, 1.9)
    expert_ids = draw_expert_ids(jax.random.fold_in(key_of[14], 71), 0)
    gate_units = draw_gate_units(jax.random.fold_in(key_of[14], 71), 0)
    slot_index = draw_slot_index(jax.random.fold_in(key_of[14], 71), 0)
    weight_in = normal_values(key_of[12], (D, EXPERTS * FF), D ** -0.5, 0.1875, ((1, 512),))
    weight_out = normal_values(key_of[13], (EXPERTS * FF, D), FF ** -0.5, 0.09375, ((0, 512),))
    return dict(query_rows=query_rows, key_rows=key_rows, value_rows=value_rows, query_tangent=query_tangent, key_tangent=key_tangent, value_tangent=value_tangent, stream=stream, stream_tangent=stream_tangent, norm_gain=norm_gain, expert_ids=expert_ids, gate_units=gate_units, slot_index=slot_index, weight_in=weight_in, weight_out=weight_out)


epsilon = 1e-06
gelu_coef = 0.7978845608028654
cubic_coef = 0.044715

def gelu_pair(inputs, tangent):
    inner_arg = gelu_coef * (inputs + cubic_coef * inputs * inputs * inputs)
    hyperbolic = jnp.tanh(inner_arg)
    values = 0.5 * inputs * (1.0 + hyperbolic)
    slopes = 0.5 * (1.0 + hyperbolic) + 0.5 * inputs * (1.0 - hyperbolic * hyperbolic) * gelu_coef * (1.0 + 3.0 * cubic_coef * inputs * inputs)
    return (values, slopes * tangent)

def head_attention(operands):
    query_head, keys_head, values_head, query_drift, keys_drift, values_drift = operands
    score_scale = HEAD_DIM ** (-0.5)
    scores = jnp.dot(query_head, keys_head.T, preferred_element_type=jnp.float32) * score_scale
    score_drift = (jnp.dot(query_drift, keys_head.T, preferred_element_type=jnp.float32) + jnp.dot(query_head, keys_drift.T, preferred_element_type=jnp.float32)) * score_scale
    probabilities = jax.nn.softmax(scores, axis=1)
    weights_low = probabilities.astype(jnp.bfloat16)
    drifted = probabilities * score_drift
    drifted_low = drifted.astype(jnp.bfloat16)
    attended = jnp.dot(weights_low, values_head, preferred_element_type=jnp.float32)
    drift_mean = lax.optimization_barrier(jnp.sum(drifted, axis=1, keepdims=True))
    attended_drift = jnp.dot(drifted_low, values_head, preferred_element_type=jnp.float32) - drift_mean * attended + jnp.dot(weights_low, values_drift, preferred_element_type=jnp.float32)
    return (attended.astype(jnp.bfloat16), attended_drift.astype(jnp.bfloat16))

def split_heads(matrix):
    return matrix.reshape(N_EXP, GROUP, HEADS, HEAD_DIM).transpose(0, 2, 1, 3).reshape(N_EXP * HEADS, GROUP, HEAD_DIM)

def join_heads(matrix):
    return matrix.reshape(N_EXP, HEADS, GROUP, HEAD_DIM).transpose(0, 2, 1, 3).reshape(TOKENS, D)

def reference(query_rows, key_rows, value_rows, query_tangent, key_tangent, value_tangent, stream, stream_tangent, norm_gain, expert_ids, gate_units, slot_index, weight_in, weight_out):
    stacked = tuple((split_heads(matrix) for matrix in (query_rows, key_rows, value_rows, query_tangent, key_tangent, value_tangent)))
    attended, attended_drift = lax.map(head_attention, stacked)
    attended = join_heads(attended)
    attended_drift = join_heads(attended_drift)
    residual_state = stream.astype(jnp.float32) + attended.astype(jnp.float32)
    state_tangent = stream_tangent.astype(jnp.float32) + attended_drift.astype(jnp.float32)
    inverse = lax.rsqrt(lax.optimization_barrier(jnp.mean(residual_state * residual_state, axis=1, keepdims=True)) + epsilon)
    cross_mean = lax.optimization_barrier(jnp.mean(residual_state * state_tangent, axis=1, keepdims=True))
    normed = (norm_gain * residual_state * inverse).astype(jnp.bfloat16)
    normed_tangent = (norm_gain * inverse * (state_tangent - residual_state * cross_mean * inverse * inverse)).astype(jnp.bfloat16)
    block_count = TOKENS // TOK_DEV
    token_ids = lax.broadcasted_iota(jnp.int32, (TOKENS, 2), 0)
    group_ids = token_ids // TOK_DEV
    kept_mask = slot_index >= 0
    slot_target = jnp.where(kept_mask, slot_index, CAP).astype(jnp.int32)
    slot_table = jnp.full((EXPERTS, block_count, CAP), TOKENS, jnp.int32)
    slot_table = slot_table.at[expert_ids, group_ids, slot_target].set(token_ids, mode='drop')
    padded = jnp.concatenate((normed, jnp.zeros((1, D), jnp.bfloat16)), axis=0)
    padded_tangent = jnp.concatenate((normed_tangent, jnp.zeros((1, D), jnp.bfloat16)), axis=0)
    block_total = FF // SLICE

    def run_expert(operands):
        expert, row_ids = operands
        inputs = padded[row_ids]
        input_drift = padded_tangent[row_ids]
        weight_first = lax.dynamic_slice_in_dim(weight_in, expert * FF, FF, 1)
        weight_second = lax.dynamic_slice_in_dim(weight_out, expert * FF, FF, 0)
        hidden_pre = jnp.dot(inputs, weight_first, preferred_element_type=jnp.float32)
        hidden_drift = jnp.dot(input_drift, weight_first, preferred_element_type=jnp.float32)
        activated, activated_drift = gelu_pair(hidden_pre, hidden_drift)
        results = []
        for source in (activated, activated_drift):
            rounded = source.astype(jnp.bfloat16)
            total = jnp.zeros((rounded.shape[0], D), jnp.float32)
            for block in range(block_total):
                partial_out = jnp.dot(rounded[:, block * SLICE:(block + 1) * SLICE], weight_second[block * SLICE:(block + 1) * SLICE], preferred_element_type=jnp.float32)
                total = total + partial_out.astype(jnp.bfloat16).astype(jnp.float32)
            results.append(total)
        return (results[0], results[1])
    expert_range = jnp.arange(EXPERTS, dtype=jnp.int32)
    expert_outs, expert_drifts = lax.map(run_expert, (expert_range, slot_table.reshape(EXPERTS, block_count * CAP)))
    flat_index = (expert_ids * (block_count * CAP) + group_ids * CAP + jnp.where(kept_mask, slot_index, 0)).astype(jnp.int32)
    gate_values = jnp.where(kept_mask, gate_units.astype(jnp.float32) / 65536.0, 0.0)
    picked = expert_outs.reshape(-1, D)[flat_index]
    picked_drift = expert_drifts.reshape(-1, D)[flat_index]
    expert_mix = lax.optimization_barrier(jnp.sum(gate_values[:, :, None] * picked, axis=1))
    mix_drift = lax.optimization_barrier(jnp.sum(gate_values[:, :, None] * picked_drift, axis=1))
    block_out = (residual_state + expert_mix).astype(jnp.bfloat16)
    block_tangent = (state_tangent + mix_drift).astype(jnp.bfloat16)
    return (block_out, block_tangent)
```

```python
import functools

import jax
import jax.numpy as jnp
from jax import lax
from jax.experimental import pallas as pl
from jax.experimental.pallas import tpu as pltpu
from jax.sharding import PartitionSpec as P

MESH = pl.DeviceIdType.MESH
HEAD_DIM = 64
BF16 = jnp.bfloat16
F32 = jnp.float32

epsilon = 1e-06
gelu_coef = 0.7978845608028654
cubic_coef = 0.044715


def gelu_pair(inputs, tangent):
    inner_arg = gelu_coef * (inputs + cubic_coef * inputs * inputs * inputs)
    hyperbolic = jnp.tanh(inner_arg)
    values = 0.5 * inputs * (1.0 + hyperbolic)
    slopes = 0.5 * (1.0 + hyperbolic) + 0.5 * inputs * (
        1.0 - hyperbolic * hyperbolic
    ) * gelu_coef * (1.0 + 3.0 * cubic_coef * inputs * inputs)
    return (values, slopes * tangent)


def dot(a, b):
    return jnp.dot(a, b, preferred_element_type=F32)


def attention_kernel(
    n,
    q,
    k,
    v,
    dq,
    dk,
    dv,
    stream,
    stream_tangent,
    gain,
    state_out,
    tangent_out,
    normed_out,
    normed_tangent_out,
    x_send,
    yz_send,
    x_all,
    yz_all,
    k_top,
    k_low,
    z_low,
    o_send,
    o_all,
    x_sent,
    x_came,
    yz_sent,
    yz_came,
    o_sent,
    o_came,
):
    rows = q.shape[0]
    me = lax.axis_index("seq")
    barrier = pltpu.get_barrier_semaphore()

    def greet(j, carry):
        pl.semaphore_signal(
            barrier, inc=1, device_id={"seq": lax.rem(me + j, n)}, device_id_type=MESH
        )
        return carry

    lax.fori_loop(1, n, greet, 0)
    for h in range(n):
        cols = slice(h * HEAD_DIM, (h + 1) * HEAD_DIM)
        x_send[h] = jnp.concatenate((dq[:, cols], q[:, cols]), axis=1) * BF16(HEAD_DIM**-0.5)
        yz_send[h] = jnp.concatenate((k[:, cols], dk[:, cols], v[:, cols], dv[:, cols]), axis=1)
    pl.semaphore_wait(barrier, n - 1)

    def part(index):
        return pl.ds(pl.multiple_of(index * rows, rows), rows)

    def yz_copy(dest, slot):
        return pltpu.make_async_remote_copy(
            src_ref=yz_send.at[dest],
            dst_ref=yz_all.at[part(slot)],
            send_sem=yz_sent.at[dest],
            recv_sem=yz_came.at[slot],
            device_id={"seq": dest},
            device_id_type=MESH,
        )

    def x_copy(dest, slot):
        return pltpu.make_async_remote_copy(
            src_ref=x_send.at[dest],
            dst_ref=x_all.at[part(slot)],
            send_sem=x_sent.at[dest],
            recv_sem=x_came.at[slot],
            device_id={"seq": dest},
            device_id_type=MESH,
        )

    def o_copy(dest, slot):
        return pltpu.make_async_remote_copy(
            src_ref=o_send.at[part(dest)],
            dst_ref=o_all.at[slot],
            send_sem=o_sent.at[dest],
            recv_sem=o_came.at[slot],
            device_id={"seq": dest},
            device_id_type=MESH,
        )

    for make in (yz_copy, x_copy):

        def send(j, carry):
            make(lax.rem(me + j, n), me).start()
            make(lax.rem(me + n - j, n), me).start()
            return carry

        lax.fori_loop(1, n // 2, send, 0)
        make(lax.rem(me + n // 2, n), me).start()

    yz_all[part(me)] = yz_send[me]
    x_all[part(me)] = x_send[me]

    def yz_arrive(j, carry):
        other = lax.rem(me + j, n)
        yz_copy(other, other).wait_recv()
        return carry

    lax.fori_loop(1, n, yz_arrive, 0)
    turned = yz_all[:, : 2 * HEAD_DIM].T
    k_low[...] = turned
    k_top[:HEAD_DIM] = jnp.zeros_like(turned[:HEAD_DIM])
    k_top[HEAD_DIM:] = turned[:HEAD_DIM]
    z_low[...] = jnp.concatenate(
        (
            jnp.zeros((n * rows, HEAD_DIM), BF16),
            yz_all[:, 2 * HEAD_DIM : 3 * HEAD_DIM],
        ),
        axis=1,
    )
    per = 4
    blocks = n // per
    for i in range(blocks):
        block = lax.rem(me // per + i, blocks)
        for u in range(per):
            other = block * per + u

            @pl.when(other != me)
            def _():
                x_copy(other, other).wait_recv()

        span = pl.ds(pl.multiple_of(block * per * rows, per * rows), per * rows)
        x = x_all[span]
        scores = dot(x, k_top[...])
        drift = dot(x, k_low[...])
        weights = jnp.exp(scores - jnp.max(scores, axis=1, keepdims=True))
        weights = weights * (1.0 / jnp.sum(weights, axis=1, keepdims=True))
        drifted = weights * drift
        mean = jnp.sum(drifted, axis=1, keepdims=True)
        both = dot(weights.astype(BF16), yz_all[:, 2 * HEAD_DIM :])
        low = dot(drifted.astype(BF16), z_low[...])
        attended = both[:, :HEAD_DIM]
        moved = low[:, HEAD_DIM:] - mean * attended + both[:, HEAD_DIM:]
        o_send[span] = jnp.concatenate((attended, moved), axis=1).astype(BF16)
        for u in range(per):
            other = block * per + u

            @pl.when(other != me)
            def _():
                o_copy(other, me).start()

    o_all[me] = o_send[part(me)]

    def o_arrive(j, carry):
        other = lax.rem(me + j, n)
        o_copy(other, other).wait_recv()
        return carry

    lax.fori_loop(1, n, o_arrive, 0)
    for h in range(0, n, 2):
        cols = slice(h * HEAD_DIM, (h + 2) * HEAD_DIM)
        first = o_all[h].astype(F32)
        second = o_all[h + 1].astype(F32)
        state_out[:, cols] = stream[:, cols].astype(F32) + jnp.concatenate(
            (first[:, :HEAD_DIM], second[:, :HEAD_DIM]), axis=1
        )
        tangent_out[:, cols] = stream_tangent[:, cols].astype(F32) + jnp.concatenate(
            (first[:, HEAD_DIM:], second[:, HEAD_DIM:]), axis=1
        )
    state = state_out[...]
    tangent = tangent_out[...]
    inverse = lax.rsqrt(jnp.mean(state * state, axis=1, keepdims=True) + epsilon)
    cross = jnp.mean(state * tangent, axis=1, keepdims=True)
    normed_out[...] = (gain[...] * state * inverse).astype(BF16)
    normed_tangent_out[...] = (
        gain[...] * inverse * (tangent - state * cross * inverse * inverse)
    ).astype(BF16)

    def drain(j, carry):
        other = lax.rem(me + j, n)
        yz_copy(other, me).wait_send()
        x_copy(other, me).wait_send()
        o_copy(other, me).wait_send()
        return carry

    lax.fori_loop(1, n, drain, 0)


def attend(q, k, v, dq, dk, dv, stream, stream_tangent, gain):
    n = lax.axis_size("seq")
    rows, width = stream.shape
    total = n * rows
    vmem = pl.BlockSpec(memory_space=pltpu.VMEM)
    dma = pltpu.SemaphoreType.DMA
    return pl.pallas_call(
        functools.partial(attention_kernel, n),
        out_shape=(
            jax.ShapeDtypeStruct((rows, width), F32),
            jax.ShapeDtypeStruct((rows, width), F32),
            jax.ShapeDtypeStruct((rows, width), BF16),
            jax.ShapeDtypeStruct((rows, width), BF16),
        ),
        in_specs=[vmem] * 9,
        out_specs=(vmem,) * 4,
        scratch_shapes=[
            pltpu.VMEM((n, rows, 2 * HEAD_DIM), BF16),
            pltpu.VMEM((n, rows, 4 * HEAD_DIM), BF16),
            pltpu.VMEM((total, 2 * HEAD_DIM), BF16),
            pltpu.VMEM((total, 4 * HEAD_DIM), BF16),
            pltpu.VMEM((2 * HEAD_DIM, total), BF16),
            pltpu.VMEM((2 * HEAD_DIM, total), BF16),
            pltpu.VMEM((total, 2 * HEAD_DIM), BF16),
            pltpu.VMEM((total, 2 * HEAD_DIM), BF16),
            pltpu.VMEM((n, rows, 2 * HEAD_DIM), BF16),
        ]
        + [dma((n,))] * 6,
        compiler_params=pltpu.CompilerParams(
            collective_id=0, has_side_effects=True, vmem_limit_bytes=48 * 1024 * 1024
        ),
        name="attend",
    )(q, k, v, dq, dk, dv, stream, stream_tangent, gain.reshape(1, width))


def per_device(
    query_rows,
    key_rows,
    value_rows,
    query_tangent,
    key_tangent,
    value_tangent,
    stream,
    stream_tangent,
    norm_gain,
    expert_ids,
    gate_units,
    slot_index,
    weight_in,
    weight_out,
):
    exp_count = lax.axis_size("exp")
    local_rows = stream.shape[0]
    model_width = stream.shape[1]
    expert_count = exp_count // 2
    capacity = 2 * ((5 * local_rows + 4 * expert_count - 1) // (4 * expert_count))
    residual_state, state_tangent, normed, normed_tangent = attend(
        query_rows,
        key_rows,
        value_rows,
        query_tangent,
        key_tangent,
        value_tangent,
        stream,
        stream_tangent,
        norm_gain,
    )
    slot_count = expert_count * capacity
    kept_mask = slot_index >= 0
    slot_codes = jnp.where(kept_mask, expert_ids * capacity + slot_index, slot_count)
    row_numbers = lax.broadcasted_iota(jnp.int32, slot_index.shape, 0)
    slot_table = (
        jnp.full((slot_count,), local_rows, jnp.int32).at[slot_codes].set(row_numbers, mode="drop")
    )
    padded = jnp.concatenate((normed, jnp.zeros((1, model_width), jnp.bfloat16)), axis=0)
    padded_tangent = jnp.concatenate(
        (normed_tangent, jnp.zeros((1, model_width), jnp.bfloat16)), axis=0
    )
    packed = padded[slot_table]
    packed_tangent = padded_tangent[slot_table]
    outgoing = jnp.repeat(packed.reshape(expert_count, capacity, model_width), 2, axis=0)
    outgoing_tangent = jnp.repeat(
        packed_tangent.reshape(expert_count, capacity, model_width), 2, axis=0
    )
    arrived, arrived_tangent = (
        lax.all_to_all(outgoing, "exp", split_axis=0, concat_axis=0, tiled=True),
        lax.all_to_all(outgoing_tangent, "exp", split_axis=0, concat_axis=0, tiled=True),
    )
    stacked_rows = jnp.stack(
        (arrived.reshape(-1, model_width), arrived_tangent.reshape(-1, model_width))
    )
    hidden_pair = jnp.einsum(
        "prd,dn->prn",
        stacked_rows,
        lax.all_gather(weight_in, "seq", axis=1, tiled=True),
        preferred_element_type=jnp.float32,
    )
    activated, activated_drift = gelu_pair(hidden_pair[0], hidden_pair[1])
    activated_pair = jnp.stack(
        (activated.astype(jnp.bfloat16), activated_drift.astype(jnp.bfloat16))
    )
    projected = jnp.einsum(
        "prn,nd->prd",
        activated_pair,
        lax.all_gather(weight_out, "seq", axis=0, tiled=True),
        preferred_element_type=jnp.float32,
    )
    projected_low = projected.astype(jnp.bfloat16)
    partial_out = projected_low[0].reshape(arrived.shape)
    partial_drift = projected_low[1].reshape(arrived.shape)
    returned, returned_tangent = (
        lax.all_to_all(partial_out, "exp", split_axis=0, concat_axis=0, tiled=True),
        lax.all_to_all(partial_drift, "exp", split_axis=0, concat_axis=0, tiled=True),
    )
    expert_sums = jnp.sum(
        returned.astype(jnp.float32).reshape(expert_count, 2, capacity, model_width), axis=1
    ).reshape(slot_count, model_width)
    expert_drifts = jnp.sum(
        returned_tangent.astype(jnp.float32).reshape(expert_count, 2, capacity, model_width), axis=1
    ).reshape(slot_count, model_width)
    flat_index = jnp.where(kept_mask, slot_codes, 0)
    gate_values = jnp.where(kept_mask, gate_units.astype(jnp.float32) / 65536.0, 0.0)
    expert_mix = jnp.sum(gate_values[:, :, None] * expert_sums[flat_index], axis=1)
    mix_drift = jnp.sum(gate_values[:, :, None] * expert_drifts[flat_index], axis=1)
    return (
        (residual_state + expert_mix).astype(jnp.bfloat16),
        (state_tangent + mix_drift).astype(jnp.bfloat16),
    )


def solution(mesh):
    rows = P(("exp", "seq"), None)
    return jax.shard_map(
        per_device,
        mesh=mesh,
        in_specs=(rows,) * 8 + (P(),) + (rows,) * 3 + (P(None, ("exp", "seq")), rows),
        out_specs=(rows, rows),
        check_vma=False,
    )
```

```python
import functools

import jax
import jax.numpy as jnp
from jax import lax
from jax.experimental import pallas as pl
from jax.experimental.pallas import tpu as pltpu
from jax.sharding import PartitionSpec as P

MESH = pl.DeviceIdType.MESH
HEAD_DIM = 64
BF16 = jnp.bfloat16
F32 = jnp.float32

epsilon = 1e-06
gelu_coef = 0.7978845608028654
cubic_coef = 0.044715


def gelu_pair(inputs, tangent):
    inner_arg = gelu_coef * (inputs + cubic_coef * inputs * inputs * inputs)
    hyperbolic = jnp.tanh(inner_arg)
    values = 0.5 * inputs * (1.0 + hyperbolic)
    slopes = 0.5 * (1.0 + hyperbolic) + 0.5 * inputs * (
        1.0 - hyperbolic * hyperbolic
    ) * gelu_coef * (1.0 + 3.0 * cubic_coef * inputs * inputs)
    return (values, slopes * tangent)


def dot(a, b):
    return jnp.dot(a, b, preferred_element_type=F32)


def one_hot(rows, columns):
    return jnp.where(rows == columns, 1.0, 0.0).astype(BF16)


def iota(shape, dim):
    return lax.broadcasted_iota(jnp.int32, shape, dim)


def ring_order(count):
    order = []
    for j in range(1, count // 2):
        order += [j, count - j]
    return order + [count // 2]


X_SIZE = 4
CHUNK = 256


def front_kernel(
    n,
    y_size,
    capacity,
    q_in,
    k_in,
    v_in,
    dq_in,
    dk_in,
    dv_in,
    stream_in,
    stream_tangent_in,
    gain,
    ids,
    slots,
    state_out,
    tangent_out,
    rows_out,
    fetched,
    fetch_sem,
    x_send,
    yz_send,
    x_all,
    yz_all,
    k_top,
    k_low,
    z_low,
    o_send,
    o_all,
    pick,
    sort,
    tokens,
    message,
    middle,
    landed,
    x_sent,
    x_came,
    yz_sent,
    yz_came,
    o_sent,
    o_came,
    m_sent,
    m_came,
    f_sent,
    f_came,
):
    sources = (q_in, k_in, v_in, dq_in, dk_in, dv_in, stream_in, stream_tangent_in)
    fetches = [
        pltpu.make_async_copy(source, fetched.at[i], fetch_sem.at[i])
        for i, source in enumerate(sources)
    ]
    for copy in fetches:
        copy.start()
    rows, width = stream_in.shape
    me = lax.axis_index("seq")
    place = lax.axis_index("exp")
    my_x, my_y = lax.rem(place, X_SIZE), place // X_SIZE
    barrier = pltpu.get_barrier_semaphore()

    def at_y(y):
        return {"exp": y * X_SIZE + my_x}

    def at_x(x):
        return {"exp": my_y * X_SIZE + x}

    def greet(j, carry):
        pl.semaphore_signal(
            barrier, inc=1, device_id={"seq": lax.rem(me + j, n)}, device_id_type=MESH
        )
        return carry

    lax.fori_loop(1, n, greet, 0)
    for j in range(1, y_size):
        pl.semaphore_signal(
            barrier, inc=1, device_id=at_y(lax.rem(my_y + j, y_size)), device_id_type=MESH
        )
    for j in range(1, X_SIZE):
        pl.semaphore_signal(
            barrier, inc=1, device_id=at_x(lax.rem(my_x + j, X_SIZE)), device_id_type=MESH
        )
    for copy in fetches[:6]:
        copy.wait()
    for h in range(n):
        cols = slice(h * HEAD_DIM, (h + 1) * HEAD_DIM)
        q, k, v, dq, dk, dv = (fetched[i, :, cols] for i in range(6))
        x_send[h] = jnp.concatenate((dq, q), axis=1) * BF16(HEAD_DIM**-0.5)
        yz_send[h] = jnp.concatenate((k, dk, v, dv), axis=1)
    pl.semaphore_wait(barrier, n - 1 + y_size - 1 + X_SIZE - 1)

    def part(index):
        return pl.ds(pl.multiple_of(index * rows, rows), rows)

    def yz_copy(dest, slot):
        return pltpu.make_async_remote_copy(
            src_ref=yz_send.at[dest],
            dst_ref=yz_all.at[part(slot)],
            send_sem=yz_sent.at[dest],
            recv_sem=yz_came.at[slot],
            device_id={"seq": dest},
            device_id_type=MESH,
        )

    def x_copy(dest, slot):
        return pltpu.make_async_remote_copy(
            src_ref=x_send.at[dest],
            dst_ref=x_all.at[part(slot)],
            send_sem=x_sent.at[dest],
            recv_sem=x_came.at[slot],
            device_id={"seq": dest},
            device_id_type=MESH,
        )

    def o_copy(dest, slot):
        return pltpu.make_async_remote_copy(
            src_ref=o_send.at[part(dest)],
            dst_ref=o_all.at[slot],
            send_sem=o_sent.at[dest],
            recv_sem=o_came.at[slot],
            device_id={"seq": dest},
            device_id_type=MESH,
        )

    for make in (yz_copy, x_copy):

        def send(j, carry):
            make(lax.rem(me + j, n), me).start()
            make(lax.rem(me + n - j, n), me).start()
            return carry

        lax.fori_loop(1, n // 2, send, 0)
        make(lax.rem(me + n // 2, n), me).start()

    yz_all[part(me)] = yz_send[me]
    x_all[part(me)] = x_send[me]

    chunks = width // CHUNK
    experts = 2 * y_size
    codes = jnp.where(slots[...] >= 0, ids[...] * capacity + slots[...], -1)
    span_codes = experts * capacity
    wide = []
    for choice in range(2):
        column = jnp.broadcast_to(codes[:, choice : choice + 1].astype(F32), (rows, 128))
        row = column.T[:1].astype(jnp.int32)
        wide.append(
            jnp.concatenate(
                [jnp.where(row >= 0, row + span_codes * i, -1) for i in range(2 * chunks)], axis=1
            )
        )
    depth = 2 * capacity * chunks
    line = iota((depth, 1), 0)
    kind = line // capacity
    wanted = lax.rem(line, capacity) + span_codes * kind

    def choose(expert, carry):
        target = wanted + expert * capacity
        hit = (target == wide[0]) | (target == wide[1])
        pick[pl.ds(pl.multiple_of(expert * depth, depth), depth)] = jnp.where(
            hit, 1.0, 0.0
        ).astype(BF16)
        return carry

    lax.fori_loop(0, experts, choose, 0)
    half = y_size // 2
    size = half * depth
    line = iota((size, 1), 0)
    kind = line // (half * capacity)
    inner = lax.rem(line, half * capacity)
    sort[...] = one_hot(
        (inner // capacity) * depth + kind * capacity + lax.rem(inner, capacity),
        iota((size, size), 1),
    )

    def yz_arrive(j, carry):
        other = lax.rem(me + j, n)
        yz_copy(other, other).wait_recv()
        return carry

    lax.fori_loop(1, n, yz_arrive, 0)
    turned = yz_all[:, : 2 * HEAD_DIM].T
    k_low[...] = turned
    k_top[:HEAD_DIM] = jnp.zeros_like(turned[:HEAD_DIM])
    k_top[HEAD_DIM:] = turned[:HEAD_DIM]
    z_low[...] = jnp.concatenate(
        (
            jnp.zeros((n * rows, HEAD_DIM), BF16),
            yz_all[:, 2 * HEAD_DIM : 3 * HEAD_DIM],
        ),
        axis=1,
    )
    per = 4
    blocks = n // per
    for i in range(blocks):
        block = lax.rem(me // per + i, blocks)
        for u in range(per):
            other = block * per + u

            @pl.when(other != me)
            def _():
                x_copy(other, other).wait_recv()

        span = pl.ds(pl.multiple_of(block * per * rows, per * rows), per * rows)
        x = x_all[span]
        scores = dot(x, k_top[...])
        drift = dot(x, k_low[...])
        weights = jnp.exp(scores - jnp.max(scores, axis=1, keepdims=True))
        weights = weights * (1.0 / jnp.sum(weights, axis=1, keepdims=True))
        drifted = weights * drift
        mean = jnp.sum(drifted, axis=1, keepdims=True)
        both = dot(weights.astype(BF16), yz_all[:, 2 * HEAD_DIM :])
        low = dot(drifted.astype(BF16), z_low[...])
        attended = both[:, :HEAD_DIM]
        moved = low[:, HEAD_DIM:] - mean * attended + both[:, HEAD_DIM:]
        o_send[span] = jnp.concatenate((attended, moved), axis=1).astype(BF16)
        for u in range(per):
            other = block * per + u

            @pl.when(other != me)
            def _():
                o_copy(other, me).start()

    o_all[me] = o_send[part(me)]
    for copy in fetches[6:]:
        copy.wait()

    def o_arrive(j, carry):
        other = lax.rem(me + j, n)
        o_copy(other, other).wait_recv()
        return carry

    lax.fori_loop(1, n, o_arrive, 0)
    for h in range(0, n, 2):
        cols = slice(h * HEAD_DIM, (h + 2) * HEAD_DIM)
        first = o_all[h].astype(F32)
        second = o_all[h + 1].astype(F32)
        state_out[:, cols] = fetched[6, :, cols].astype(F32) + jnp.concatenate(
            (first[:, :HEAD_DIM], second[:, :HEAD_DIM]), axis=1
        )
        tangent_out[:, cols] = fetched[7, :, cols].astype(F32) + jnp.concatenate(
            (first[:, HEAD_DIM:], second[:, HEAD_DIM:]), axis=1
        )
    state = state_out[...]
    tangent = tangent_out[...]
    inverse = lax.rsqrt(jnp.mean(state * state, axis=1, keepdims=True) + epsilon)
    cross = jnp.mean(state * tangent, axis=1, keepdims=True)
    normed = (gain[...] * state * inverse).astype(BF16)
    normed_tangent = (
        gain[...] * inverse * (tangent - state * cross * inverse * inverse)
    ).astype(BF16)
    for c in range(chunks):
        cols = slice(c * CHUNK, (c + 1) * CHUNK)
        tokens[2 * c * rows : (2 * c + 1) * rows] = normed[:, cols]
        tokens[(2 * c + 1) * rows : (2 * c + 2) * rows] = normed_tangent[:, cols]

    def m_copy(dest, slot):
        return pltpu.make_async_remote_copy(
            src_ref=message.at[dest],
            dst_ref=middle.at[slot],
            send_sem=m_sent.at[dest],
            recv_sem=m_came.at[slot],
            device_id=at_y(dest),
            device_id_type=MESH,
        )

    def f_copy(dest, source_x, source_y):
        pair = pl.ds(pl.multiple_of((dest // 2) * depth, depth), depth)
        return pltpu.make_async_remote_copy(
            src_ref=middle.at[source_y, pair],
            dst_ref=landed.at[source_x, source_y],
            send_sem=f_sent.at[dest, source_y],
            recv_sem=f_came.at[source_x, source_y],
            device_id=at_x(dest),
            device_id_type=MESH,
        )

    def fill(dest):
        picked = pick[pl.ds(pl.multiple_of(dest * 2 * depth, 2 * depth), 2 * depth)]
        return dot(picked, tokens[...]).astype(BF16)

    def spread(source_y):
        for j in (1, 3, 2):
            f_copy(lax.rem(my_x + j, X_SIZE), my_x, source_y).start()
        landed[my_x, source_y] = middle[
            source_y, pl.ds(pl.multiple_of((my_x // 2) * depth, depth), depth)
        ]

    order = ring_order(y_size)
    for j in order:
        dest = lax.rem(my_y + j, y_size)
        message[dest] = fill(dest)
        m_copy(dest, my_y).start()
    middle[my_y] = fill(my_y)
    spread(my_y)
    for j in order:
        other = lax.rem(my_y + j, y_size)
        m_copy(other, other).wait_recv()
        spread(other)
    for j in [0] + order:
        other = lax.rem(my_y + j, y_size)
        for i in range(1, X_SIZE):
            source = lax.rem(my_x + i, X_SIZE)
            f_copy(source, source, other).wait_recv()
    group = half * capacity
    for x in range(X_SIZE):
        sorted_rows = [
            dot(sort[...], landed[x, side * half : (side + 1) * half].reshape(size, CHUNK))
            for side in range(2)
        ]
        for c in range(chunks):
            for tangent_kind in range(2):
                top = (2 * c + tangent_kind) * group
                rows_out[
                    pl.ds((tangent_kind * X_SIZE + x) * 2 * group, 2 * group),
                    pl.ds(c * CHUNK, CHUNK),
                ] = jnp.concatenate(
                    [values[top : top + group] for values in sorted_rows], axis=0
                ).astype(BF16)

    def drain(j, carry):
        other = lax.rem(me + j, n)
        yz_copy(other, me).wait_send()
        x_copy(other, me).wait_send()
        o_copy(other, me).wait_send()
        return carry

    lax.fori_loop(1, n, drain, 0)
    for j in order:
        m_copy(lax.rem(my_y + j, y_size), my_y).wait_send()
    for y in range(y_size):
        for j in range(1, X_SIZE):
            f_copy(lax.rem(my_x + j, X_SIZE), my_x, y).wait_send()


def front(arrays, gain, ids, slots, capacity):
    n = lax.axis_size("seq")
    y_size = lax.axis_size("exp") // X_SIZE
    rows, width = arrays[0].shape
    total = n * rows
    chunks = width // CHUNK
    depth = 2 * capacity * chunks
    vmem = pl.BlockSpec(memory_space=pltpu.VMEM)
    away = pl.BlockSpec(memory_space=pl.ANY)
    dma = pltpu.SemaphoreType.DMA
    return pl.pallas_call(
        functools.partial(front_kernel, n, y_size, capacity),
        out_shape=(
            jax.ShapeDtypeStruct((rows, width), F32),
            jax.ShapeDtypeStruct((rows, width), F32),
            jax.ShapeDtypeStruct((2 * X_SIZE * y_size * capacity, width), BF16),
        ),
        in_specs=[away] * 8 + [vmem] * 3,
        out_specs=(vmem,) * 3,
        scratch_shapes=[
            pltpu.VMEM((8, rows, width), BF16),
            dma((8,)),
            pltpu.VMEM((n, rows, 2 * HEAD_DIM), BF16),
            pltpu.VMEM((n, rows, 4 * HEAD_DIM), BF16),
            pltpu.VMEM((total, 2 * HEAD_DIM), BF16),
            pltpu.VMEM((total, 4 * HEAD_DIM), BF16),
            pltpu.VMEM((2 * HEAD_DIM, total), BF16),
            pltpu.VMEM((2 * HEAD_DIM, total), BF16),
            pltpu.VMEM((total, 2 * HEAD_DIM), BF16),
            pltpu.VMEM((total, 2 * HEAD_DIM), BF16),
            pltpu.VMEM((n, rows, 2 * HEAD_DIM), BF16),
            pltpu.VMEM((2 * y_size * depth, 2 * chunks * rows), BF16),
            pltpu.VMEM((y_size // 2 * depth, y_size // 2 * depth), BF16),
            pltpu.VMEM((2 * chunks * rows, CHUNK), BF16),
            pltpu.VMEM((y_size, 2 * depth, CHUNK), BF16),
            pltpu.VMEM((y_size, 2 * depth, CHUNK), BF16),
            pltpu.VMEM((X_SIZE, y_size, depth, CHUNK), BF16),
        ]
        + [dma((n,))] * 6
        + [dma((y_size,))] * 2
        + [dma((X_SIZE, y_size))] * 2,
        compiler_params=pltpu.CompilerParams(
            collective_id=0, has_side_effects=True, vmem_limit_bytes=48 * 1024 * 1024
        ),
        name="front",
    )(*arrays, gain.reshape(1, width), ids, slots)


def back_kernel(
    n,
    y_size,
    capacity,
    rows_in,
    first_in,
    second_in,
    state,
    tangent,
    ids,
    gates,
    slots,
    out,
    out_tangent,
    first,
    second,
    active,
    sort,
    gate_high,
    gate_low,
    halves_send,
    halves,
    sums_send,
    sums,
    a_own,
    a_sent,
    a_came,
    b_own,
    b_sent,
    b_came,
    h_sent,
    h_came,
    s_sent,
    s_came,
):
    me = lax.axis_index("seq")
    core = lax.rem(me, 2)
    partner = me + 1 - 2 * core
    place = lax.axis_index("exp")
    my_x, my_y = lax.rem(place, X_SIZE), place // X_SIZE
    tokens, width = state.shape
    chunks = width // CHUNK
    shards, _, units = first_in.shape
    barrier = pltpu.get_barrier_semaphore()

    def at_y(y):
        return {"exp": y * X_SIZE + my_x}

    def at_x(x):
        return {"exp": my_y * X_SIZE + x}

    pl.semaphore_signal(barrier, inc=1, device_id={"seq": partner}, device_id_type=MESH)
    for j in range(1, X_SIZE):
        pl.semaphore_signal(
            barrier, inc=1, device_id=at_x(lax.rem(my_x + j, X_SIZE)), device_id_type=MESH
        )
    for j in range(1, y_size):
        pl.semaphore_signal(
            barrier, inc=1, device_id=at_y(lax.rem(my_y + j, y_size)), device_id_type=MESH
        )

    def first_own(j):
        return pltpu.make_async_copy(first_in.at[j], first.at[2 * j + core], a_own.at[j])

    def first_copy(j, owner):
        return pltpu.make_async_remote_copy(
            src_ref=first_in.at[j],
            dst_ref=first.at[2 * j + owner],
            send_sem=a_sent.at[j],
            recv_sem=a_came.at[j],
            device_id={"seq": partner},
            device_id_type=MESH,
        )

    def second_part(j, owner):
        return second.at[pl.ds(pl.multiple_of((2 * j + owner) * units, units), units)]

    def second_own(j):
        return pltpu.make_async_copy(second_in.at[j], second_part(j, core), b_own.at[j])

    def second_copy(j, owner):
        return pltpu.make_async_remote_copy(
            src_ref=second_in.at[j],
            dst_ref=second_part(j, owner),
            send_sem=b_sent.at[j],
            recv_sem=b_came.at[j],
            device_id={"seq": partner},
            device_id_type=MESH,
        )

    for j in range(shards):
        first_own(j).start()
    for j in range(shards):
        second_own(j).start()
    pl.semaphore_wait(barrier, 1 + X_SIZE - 1 + y_size - 1)
    for j in range(shards):
        first_copy(j, core).start()
    for j in range(shards):
        second_copy(j, core).start()

    experts = 2 * y_size
    span_codes = experts * capacity
    parts = CHUNK // 128
    depth = parts * 2 * capacity
    line = iota((1, experts * depth), 1)
    inner = lax.rem(line, depth)
    column_codes = (
        (line // depth) * capacity + lax.rem(inner, capacity) + span_codes * (inner // capacity)
    )
    high = jnp.zeros((2 * parts * tokens, experts * depth), F32)
    low = high
    for choice in range(2):
        pick = slice(choice, choice + 1)
        slot = slots[:, pick]
        code = jnp.where(slot >= 0, ids[:, pick] * capacity + slot, -1)
        code = jnp.concatenate(
            [jnp.where(code >= 0, code + span_codes * i, -1) for i in range(2 * parts)], axis=0
        )
        top = gates[:, pick] // 256
        rest = gates[:, pick] - top * 256
        top = jnp.concatenate([top.astype(F32)] * (2 * parts), axis=0)
        rest = jnp.concatenate([rest.astype(F32)] * (2 * parts), axis=0)
        hit = code == column_codes
        high = high + jnp.where(hit, top, 0.0)
        low = low + jnp.where(hit, rest, 0.0)
    gate_high[...] = high.astype(BF16)
    gate_low[...] = low.astype(BF16)
    size = parts * 2 * y_size * capacity
    line = iota((size, 1), 0)
    inner = lax.rem(line, depth)
    sort[...] = one_hot(
        (inner // capacity) * (y_size * capacity)
        + (line // depth) * capacity
        + lax.rem(inner, capacity),
        iota((size, size), 1),
    )

    count = rows_in.shape[0] // 2

    def project(j, carry):
        first_own(j).wait()
        first_copy(j, 1 - core).wait_recv()
        weights = jnp.concatenate((first[2 * j], first[2 * j + 1]), axis=1)
        hidden = dot(rows_in[...], weights)
        values, slopes = gelu_pair(hidden[:count], hidden[count:])
        cols = pl.ds(pl.multiple_of(j * 2 * units, 2 * units), 2 * units)
        active[:count, cols] = values.astype(BF16)
        active[count:, cols] = slopes.astype(BF16)
        return carry

    lax.fori_loop(0, shards, project, 0)

    def second_wait(j, carry):
        second_own(j).wait()
        second_copy(j, 1 - core).wait_recv()
        return carry

    lax.fori_loop(0, shards, second_wait, 0)

    block = y_size * capacity

    def h_copy(c, dest, slot):
        return pltpu.make_async_remote_copy(
            src_ref=halves_send.at[c, dest],
            dst_ref=halves.at[c, slot],
            send_sem=h_sent.at[c, dest],
            recv_sem=h_came.at[c, slot],
            device_id=at_x(dest),
            device_id_type=MESH,
        )

    def s_copy(c, dest, slot):
        return pltpu.make_async_remote_copy(
            src_ref=sums_send.at[c, dest],
            dst_ref=sums.at[c, slot],
            send_sem=s_sent.at[c, dest],
            recv_sem=s_came.at[c, slot],
            device_id=at_y(dest),
            device_id_type=MESH,
        )

    order = ring_order(y_size)

    def expert_block(c):
        done = dot(active[...], second[:, c * CHUNK : (c + 1) * CHUNK]).astype(BF16)
        for x in range(X_SIZE):
            halves_send[c, x, :block] = done[x * block : (x + 1) * block]
            halves_send[c, x, block:] = done[count + x * block : count + (x + 1) * block]
        for j in (1, 3, 2):
            h_copy(c, lax.rem(my_x + j, X_SIZE), my_x).start()
        halves[c, my_x] = halves_send[c, my_x]

    def return_block(c):
        for j in (1, 3, 2):
            source = lax.rem(my_x + j, X_SIZE)
            h_copy(c, source, source).wait_recv()
        pair = [
            (halves[c, 2 * p].astype(F32) + halves[c, 2 * p + 1].astype(F32)).astype(BF16)
            for p in range(2)
        ]
        stacked = jnp.concatenate(
            [
                jnp.concatenate([total[:, i * 128 : (i + 1) * 128] for total in pair], axis=1)
                for i in range(parts)
            ],
            axis=0,
        )
        ready = dot(sort[...], stacked)
        for y in range(y_size):
            piece = ready[y * depth : (y + 1) * depth]
            sums_send[c, y] = jnp.concatenate((piece[:, :128], piece[:, 128:]), axis=0).astype(
                BF16
            )
        for j in order:
            s_copy(c, lax.rem(my_y + j, y_size), my_y).start()
        sums[c, my_y] = sums_send[c, my_y]

    def mix_block(c):
        for j in order:
            source = lax.rem(my_y + j, y_size)
            s_copy(c, source, source).wait_recv()
        values = sums[c].reshape(experts * depth, 128)
        mixed = (dot(gate_high[...], values) * 256.0 + dot(gate_low[...], values)) * (
            1.0 / 65536.0
        )
        for i in range(parts):
            cols = slice(c * CHUNK + i * 128, c * CHUNK + (i + 1) * 128)
            top = 2 * i * tokens
            out[:, cols] = (state[:, cols] + mixed[top : top + tokens]).astype(BF16)
            out_tangent[:, cols] = (
                tangent[:, cols] + mixed[top + tokens : top + 2 * tokens]
            ).astype(BF16)

    for c in range(chunks):
        expert_block(c)
        if c:
            return_block(c - 1)
    return_block(chunks - 1)
    for c in range(chunks):
        mix_block(c)

    def drain(j, carry):
        first_copy(j, core).wait_send()
        second_copy(j, core).wait_send()
        return carry

    lax.fori_loop(0, shards, drain, 0)
    for c in range(chunks):
        for j in range(1, X_SIZE):
            h_copy(c, lax.rem(my_x + j, X_SIZE), my_x).wait_send()
        for j in order:
            s_copy(c, lax.rem(my_y + j, y_size), my_y).wait_send()


def back(rows_in, first_in, second_in, state, tangent, ids, gates, slots, capacity):
    n = lax.axis_size("seq")
    y_size = lax.axis_size("exp") // X_SIZE
    tokens, width = state.shape
    chunks = width // CHUNK
    shards, _, units = first_in.shape
    parts = CHUNK // 128
    depth = parts * 2 * capacity
    block = y_size * capacity
    size = parts * 2 * block
    vmem = pl.BlockSpec(memory_space=pltpu.VMEM)
    away = pl.BlockSpec(memory_space=pl.ANY)
    dma = pltpu.SemaphoreType.DMA
    return pl.pallas_call(
        functools.partial(back_kernel, n, y_size, capacity),
        out_shape=(
            jax.ShapeDtypeStruct((tokens, width), BF16),
            jax.ShapeDtypeStruct((tokens, width), BF16),
        ),
        in_specs=[vmem, away, away] + [vmem] * 5,
        out_specs=(vmem,) * 2,
        scratch_shapes=[
            pltpu.VMEM((2 * shards, width, units), BF16),
            pltpu.VMEM((2 * shards * units, width), BF16),
            pltpu.VMEM((2 * X_SIZE * block, 2 * shards * units), BF16),
            pltpu.VMEM((size, size), BF16),
            pltpu.VMEM((2 * parts * tokens, 2 * y_size * depth), BF16),
            pltpu.VMEM((2 * parts * tokens, 2 * y_size * depth), BF16),
            pltpu.VMEM((chunks, X_SIZE, 2 * block, CHUNK), BF16),
            pltpu.VMEM((chunks, X_SIZE, 2 * block, CHUNK), BF16),
            pltpu.VMEM((chunks, y_size, 2 * depth, 128), BF16),
            pltpu.VMEM((chunks, y_size, 2 * depth, 128), BF16),
        ]
        + [dma((shards,))] * 6
        + [dma((chunks, X_SIZE))] * 2
        + [dma((chunks, y_size))] * 2,
        compiler_params=pltpu.CompilerParams(
            collective_id=1, has_side_effects=True, vmem_limit_bytes=48 * 1024 * 1024
        ),
        name="back",
    )(rows_in, first_in, second_in, state, tangent, ids, gates, slots)


def per_device(
    query_rows,
    key_rows,
    value_rows,
    query_tangent,
    key_tangent,
    value_tangent,
    stream,
    stream_tangent,
    norm_gain,
    expert_ids,
    gate_units,
    slot_index,
    weight_in,
    weight_out,
):
    n = lax.axis_size("seq")
    expert_count = lax.axis_size("exp") // 2
    local_rows = stream.shape[0]
    capacity = 2 * ((5 * local_rows + 4 * expert_count - 1) // (4 * expert_count))
    same_core = [list(range(core, n, 2)) for core in range(2)]
    first = lax.all_gather(weight_in, "seq", axis_index_groups=same_core)
    second = lax.all_gather(weight_out, "seq", axis_index_groups=same_core)
    state, tangent, rows = front(
        (
            query_rows,
            key_rows,
            value_rows,
            query_tangent,
            key_tangent,
            value_tangent,
            stream,
            stream_tangent,
        ),
        norm_gain,
        expert_ids,
        slot_index,
        capacity,
    )
    return back(
        rows, first, second, state, tangent, expert_ids, gate_units, slot_index, capacity
    )


def solution(mesh):
    rows = P(("exp", "seq"), None)
    return jax.shard_map(
        per_device,
        mesh=mesh,
        in_specs=(rows,) * 8 + (P(),) + (rows,) * 3 + (P(None, ("exp", "seq")), rows),
        out_specs=(rows, rows),
        check_vma=False,
    )
```

```python
import functools

import jax
import jax.numpy as jnp
from jax import lax
from jax.experimental import pallas as pl
from jax.experimental.pallas import tpu as pltpu
from jax.sharding import PartitionSpec as P

MESH = pl.DeviceIdType.MESH
HEAD_DIM = 64
BF16 = jnp.bfloat16
F32 = jnp.float32

epsilon = 1e-06
gelu_coef = 0.7978845608028654
cubic_coef = 0.044715


def gelu_pair(inputs, tangent):
    inner_arg = gelu_coef * (inputs + cubic_coef * inputs * inputs * inputs)
    hyperbolic = jnp.tanh(inner_arg)
    values = 0.5 * inputs * (1.0 + hyperbolic)
    slopes = 0.5 * (1.0 + hyperbolic) + 0.5 * inputs * (
        1.0 - hyperbolic * hyperbolic
    ) * gelu_coef * (1.0 + 3.0 * cubic_coef * inputs * inputs)
    return (values, slopes * tangent)


def dot(a, b):
    return jnp.dot(a, b, preferred_element_type=F32)


def one_hot(rows, columns):
    return jnp.where(rows == columns, 1.0, 0.0).astype(BF16)


def iota(shape, dim):
    return lax.broadcasted_iota(jnp.int32, shape, dim)


def ring_order(count):
    order = []
    for j in range(1, count // 2):
        order += [j, count - j]
    return order + [count // 2]


X_SIZE = 4
CHUNK = 256


RING_PIECES = 6
HOPS = 4


def block_kernel(
    n,
    y_size,
    capacity,
    q_in,
    k_in,
    v_in,
    dq_in,
    dk_in,
    dv_in,
    stream_in,
    stream_tangent_in,
    gain_in,
    ids_in,
    gates_in,
    slots_in,
    first_in,
    second_in,
    out,
    out_tangent,
    fetched,
    gain,
    numbers,
    first,
    second,
    x_send,
    yz_send,
    x_all,
    yz_all,
    k_top,
    k_low,
    z_low,
    o_send,
    o_all,
    pick,
    sort,
    tokens,
    message,
    middle,
    landed,
    state,
    tangent,
    expert_rows,
    active,
    back_sort,
    gate_high,
    gate_low,
    halves_send,
    halves,
    sums_send,
    sums,
    fetch_sem,
    x_sent,
    x_came,
    yz_sent,
    yz_came,
    o_sent,
    o_came,
    m_sent,
    m_came,
    f_sent,
    f_came,
    w_sent,
    w_came,
    p_sent,
    p_came,
    h_sent,
    h_came,
    s_sent,
    s_came,
):
    rows, width = stream_in.shape
    units = first_in.shape[1]
    me = lax.axis_index("seq")
    core = lax.rem(me, 2)
    partner = me + 1 - 2 * core
    my_z = me // 2
    shards = n // 2
    place = lax.axis_index("exp")
    my_x, my_y = lax.rem(place, X_SIZE), place // X_SIZE
    chunks = width // CHUNK
    experts = 2 * y_size
    span_codes = experts * capacity
    order = ring_order(y_size)

    def at_y(y):
        return {"exp": y * X_SIZE + my_x}

    def at_x(x):
        return {"exp": my_y * X_SIZE + x}

    def part(index):
        return pl.ds(pl.multiple_of(index * rows, rows), rows)

    def unit_rows(index):
        return pl.ds(pl.multiple_of(index * units, units), units)

    sources = (q_in, k_in, v_in, dq_in, dk_in, dv_in, stream_in, stream_tangent_in)
    targets = [fetched.at[i] for i in range(8)]
    sources += (gain_in, ids_in, gates_in, slots_in, first_in, second_in)
    targets += [gain, numbers.at[0], numbers.at[1], numbers.at[2]]
    targets += [first.at[me], second.at[unit_rows(me)]]
    fetches = [
        pltpu.make_async_copy(source, target, fetch_sem.at[i])
        for i, (source, target) in enumerate(zip(sources, targets))
    ]
    for copy in fetches:
        copy.start()

    barrier = pltpu.get_barrier_semaphore()

    def greet(j, carry):
        pl.semaphore_signal(
            barrier, inc=1, device_id={"seq": lax.rem(me + j, n)}, device_id_type=MESH
        )
        return carry

    lax.fori_loop(1, n, greet, 0)
    for j in range(1, y_size):
        pl.semaphore_signal(
            barrier, inc=1, device_id=at_y(lax.rem(my_y + j, y_size)), device_id_type=MESH
        )
    for j in range(1, X_SIZE):
        pl.semaphore_signal(
            barrier, inc=1, device_id=at_x(lax.rem(my_x + j, X_SIZE)), device_id_type=MESH
        )

    def piece_at(piece, index):
        if piece < 2:
            return first.at[index, piece * (width // 2) : (piece + 1) * (width // 2)]
        cols = slice((piece - 2) * CHUNK, (piece - 1) * CHUNK)
        return second.at[unit_rows(index), cols]

    def hops(piece, way):
        return HOPS if (piece + way) % 2 == 0 else HOPS - 1

    def ring_copy(piece, way, hop, arriving):
        step = 1 if way == 0 else shards - 1
        back = hop if arriving else hop - 1
        origin = lax.rem(my_z + (shards - step) * back, shards)
        block = piece_at(piece, 2 * origin + core)
        return pltpu.make_async_remote_copy(
            src_ref=block,
            dst_ref=block,
            send_sem=w_sent.at[piece, way * HOPS + hop - 1],
            recv_sem=w_came.at[piece, way * HOPS + hop - 1],
            device_id={"seq": 2 * lax.rem(my_z + step, shards) + core},
            device_id_type=MESH,
        )

    def share_copy(piece, z, owner):
        block = piece_at(piece, 2 * z + owner)
        return pltpu.make_async_remote_copy(
            src_ref=block,
            dst_ref=block,
            send_sem=p_sent.at[piece, z],
            recv_sem=p_came.at[piece, z],
            device_id={"seq": partner},
            device_id_type=MESH,
        )

    def ring_open(piece):
        for way in range(2):
            ring_copy(piece, way, 1, False).start()
        share_copy(piece, my_z, core).start()

    def ring_step(piece, hop):
        for way in range(2):
            if hop <= hops(piece, way):
                ring_copy(piece, way, hop, True).wait_recv()
                if hop < hops(piece, way):
                    ring_copy(piece, way, hop + 1, False).start()
                step = 1 if way == 0 else shards - 1
                origin = lax.rem(my_z + (shards - step) * hop, shards)
                share_copy(piece, origin, core).start()

    for copy in fetches[:6]:
        copy.wait()
    for h in range(n):
        cols = slice(h * HEAD_DIM, (h + 1) * HEAD_DIM)
        q, k, v, dq, dk, dv = (fetched[i, :, cols] for i in range(6))
        x_send[h] = jnp.concatenate((dq, q), axis=1) * BF16(HEAD_DIM**-0.5)
        yz_send[h] = jnp.concatenate((k, dk, v, dv), axis=1)
    pl.semaphore_wait(barrier, n - 1 + y_size - 1 + X_SIZE - 1)

    def yz_copy(dest, slot):
        return pltpu.make_async_remote_copy(
            src_ref=yz_send.at[dest],
            dst_ref=yz_all.at[part(slot)],
            send_sem=yz_sent.at[dest],
            recv_sem=yz_came.at[slot],
            device_id={"seq": dest},
            device_id_type=MESH,
        )

    def x_copy(dest, slot):
        return pltpu.make_async_remote_copy(
            src_ref=x_send.at[dest],
            dst_ref=x_all.at[part(slot)],
            send_sem=x_sent.at[dest],
            recv_sem=x_came.at[slot],
            device_id={"seq": dest},
            device_id_type=MESH,
        )

    def o_copy(dest, slot):
        return pltpu.make_async_remote_copy(
            src_ref=o_send.at[part(dest)],
            dst_ref=o_all.at[slot],
            send_sem=o_sent.at[dest],
            recv_sem=o_came.at[slot],
            device_id={"seq": dest},
            device_id_type=MESH,
        )

    for make in (yz_copy, x_copy):

        def send(j, carry):
            make(lax.rem(me + j, n), me).start()
            make(lax.rem(me + n - j, n), me).start()
            return carry

        lax.fori_loop(1, n // 2, send, 0)
        make(lax.rem(me + n // 2, n), me).start()

    yz_all[part(me)] = yz_send[me]
    x_all[part(me)] = x_send[me]
    for copy in fetches[6:]:
        copy.wait()

    codes = jnp.where(numbers[2] >= 0, numbers[0] * capacity + numbers[2], -1)
    wide = [
        jnp.concatenate(
            [jnp.where(row >= 0, row + span_codes * i, -1) for i in range(2 * chunks)], axis=1
        )
        for row in (codes[:1], codes[1:])
    ]
    depth = 2 * capacity * chunks
    line = iota((depth, 1), 0)
    wanted = lax.rem(line, capacity) + span_codes * (line // capacity)

    def choose(expert, carry):
        target = wanted + expert * capacity
        hit = (target == wide[0]) | (target == wide[1])
        pick[pl.ds(pl.multiple_of(expert * depth, depth), depth)] = jnp.where(
            hit, 1.0, 0.0
        ).astype(BF16)
        return carry

    lax.fori_loop(0, experts, choose, 0)
    half = y_size // 2
    size = half * depth
    line = iota((size, 1), 0)
    inner = lax.rem(line, half * capacity)
    sort[...] = one_hot(
        (inner // capacity) * depth
        + (line // (half * capacity)) * capacity
        + lax.rem(inner, capacity),
        iota((size, size), 1),
    )

    parts = CHUNK // 128
    back_depth = parts * 2 * capacity
    line = iota((1, experts * back_depth), 1)
    inner = lax.rem(line, back_depth)
    column_codes = (
        (line // back_depth) * capacity
        + lax.rem(inner, capacity)
        + span_codes * (inner // capacity)
    )

    def upright(row):
        return jnp.broadcast_to(row.astype(F32), (128, rows)).T[:, :1].astype(jnp.int32)

    high = jnp.zeros((2 * parts * rows, experts * back_depth), F32)
    low = high
    for choice in range(2):
        code = upright(codes[choice : choice + 1])
        gate = upright(numbers[1, choice : choice + 1])
        code = jnp.concatenate(
            [jnp.where(code >= 0, code + span_codes * i, -1) for i in range(2 * parts)], axis=0
        )
        top = gate // 256
        rest = gate - top * 256
        top = jnp.concatenate([top.astype(F32)] * (2 * parts), axis=0)
        rest = jnp.concatenate([rest.astype(F32)] * (2 * parts), axis=0)
        hit = code == column_codes
        high = high + jnp.where(hit, top, 0.0)
        low = low + jnp.where(hit, rest, 0.0)
    gate_high[...] = high.astype(BF16)
    gate_low[...] = low.astype(BF16)
    back_size = parts * 2 * y_size * capacity
    line = iota((back_size, 1), 0)
    inner = lax.rem(line, back_depth)
    back_sort[...] = one_hot(
        (inner // capacity) * (y_size * capacity)
        + (line // back_depth) * capacity
        + lax.rem(inner, capacity),
        iota((back_size, back_size), 1),
    )

    def yz_arrive(j, carry):
        other = lax.rem(me + j, n)
        yz_copy(other, other).wait_recv()
        return carry

    lax.fori_loop(1, n, yz_arrive, 0)
    for piece in range(2):
        ring_open(piece)
    turned = yz_all[:, : 2 * HEAD_DIM].T
    k_low[...] = turned
    k_top[:HEAD_DIM] = jnp.zeros_like(turned[:HEAD_DIM])
    k_top[HEAD_DIM:] = turned[:HEAD_DIM]
    z_low[...] = jnp.concatenate(
        (
            jnp.zeros((n * rows, HEAD_DIM), BF16),
            yz_all[:, 2 * HEAD_DIM : 3 * HEAD_DIM],
        ),
        axis=1,
    )
    per = 4
    blocks = n // per
    for i in range(blocks):
        block = lax.rem(me // per + i, blocks)
        for u in range(per):
            other = block * per + u

            @pl.when(other != me)
            def _():
                x_copy(other, other).wait_recv()

        span = pl.ds(pl.multiple_of(block * per * rows, per * rows), per * rows)
        x = x_all[span]
        scores = dot(x, k_top[...])
        drift = dot(x, k_low[...])
        weights = jnp.exp(scores - jnp.max(scores, axis=1, keepdims=True))
        weights = weights * (1.0 / jnp.sum(weights, axis=1, keepdims=True))
        drifted = weights * drift
        mean = jnp.sum(drifted, axis=1, keepdims=True)
        both = dot(weights.astype(BF16), yz_all[:, 2 * HEAD_DIM :])
        low = dot(drifted.astype(BF16), z_low[...])
        attended = both[:, :HEAD_DIM]
        moved = low[:, HEAD_DIM:] - mean * attended + both[:, HEAD_DIM:]
        o_send[span] = jnp.concatenate((attended, moved), axis=1).astype(BF16)
        for u in range(per):
            other = block * per + u

            @pl.when(other != me)
            def _():
                o_copy(other, me).start()

    o_all[me] = o_send[part(me)]
    ring_step(0, 1)
    ring_step(1, 1)

    def o_arrive(j, carry):
        other = lax.rem(me + j, n)
        o_copy(other, other).wait_recv()
        return carry

    lax.fori_loop(1, n, o_arrive, 0)
    ring_step(0, 2)
    ring_step(1, 2)
    ring_open(2)
    ring_open(3)
    for h in range(0, n, 2):
        cols = slice(h * HEAD_DIM, (h + 2) * HEAD_DIM)
        one = o_all[h].astype(F32)
        two = o_all[h + 1].astype(F32)
        state[:, cols] = fetched[6, :, cols].astype(F32) + jnp.concatenate(
            (one[:, :HEAD_DIM], two[:, :HEAD_DIM]), axis=1
        )
        tangent[:, cols] = fetched[7, :, cols].astype(F32) + jnp.concatenate(
            (one[:, HEAD_DIM:], two[:, HEAD_DIM:]), axis=1
        )
    wide_state = state[...]
    wide_tangent = tangent[...]
    inverse = lax.rsqrt(jnp.mean(wide_state * wide_state, axis=1, keepdims=True) + epsilon)
    cross = jnp.mean(wide_state * wide_tangent, axis=1, keepdims=True)
    normed = (gain[...] * wide_state * inverse).astype(BF16)
    normed_tangent = (
        gain[...] * inverse * (wide_tangent - wide_state * cross * inverse * inverse)
    ).astype(BF16)
    for c in range(chunks):
        cols = slice(c * CHUNK, (c + 1) * CHUNK)
        tokens[2 * c * rows : (2 * c + 1) * rows] = normed[:, cols]
        tokens[(2 * c + 1) * rows : (2 * c + 2) * rows] = normed_tangent[:, cols]

    def m_copy(dest, slot):
        return pltpu.make_async_remote_copy(
            src_ref=message.at[dest],
            dst_ref=middle.at[slot],
            send_sem=m_sent.at[dest],
            recv_sem=m_came.at[slot],
            device_id=at_y(dest),
            device_id_type=MESH,
        )

    def f_copy(dest, source_x, source_y):
        pair = pl.ds(pl.multiple_of((dest // 2) * depth, depth), depth)
        return pltpu.make_async_remote_copy(
            src_ref=middle.at[source_y, pair],
            dst_ref=landed.at[source_x, source_y],
            send_sem=f_sent.at[dest, source_y],
            recv_sem=f_came.at[source_x, source_y],
            device_id=at_x(dest),
            device_id_type=MESH,
        )

    def fill(dest):
        picked = pick[pl.ds(pl.multiple_of(dest * 2 * depth, 2 * depth), 2 * depth)]
        return dot(picked, tokens[...]).astype(BF16)

    def spread(source_y):
        for j in (1, 3, 2):
            f_copy(lax.rem(my_x + j, X_SIZE), my_x, source_y).start()
        landed[my_x, source_y] = middle[
            source_y, pl.ds(pl.multiple_of((my_x // 2) * depth, depth), depth)
        ]

    for j in order:
        dest = lax.rem(my_y + j, y_size)
        message[dest] = fill(dest)
        m_copy(dest, my_y).start()
    middle[my_y] = fill(my_y)
    spread(my_y)
    for i, j in enumerate(order):
        other = lax.rem(my_y + j, y_size)
        m_copy(other, other).wait_recv()
        spread(other)
        if i in (1, 4):
            for piece in range(2):
                ring_step(piece, 3 if i == 1 else 4)
        if i == 5:
            ring_step(2, 1)
            ring_step(3, 1)
            ring_open(4)
            ring_open(5)
    for j in [0] + order:
        other = lax.rem(my_y + j, y_size)
        for i in range(1, X_SIZE):
            source = lax.rem(my_x + i, X_SIZE)
            f_copy(source, source, other).wait_recv()
    group = half * capacity
    for x in range(X_SIZE):
        sorted_rows = [
            dot(sort[...], landed[x, side * half : (side + 1) * half].reshape(size, CHUNK))
            for side in range(2)
        ]
        for c in range(chunks):
            for kind in range(2):
                top = (2 * c + kind) * group
                expert_rows[
                    pl.ds((kind * X_SIZE + x) * 2 * group, 2 * group),
                    pl.ds(c * CHUNK, CHUNK),
                ] = jnp.concatenate(
                    [values[top : top + group] for values in sorted_rows], axis=0
                ).astype(BF16)
    ring_step(2, 2)
    ring_step(3, 2)

    count = X_SIZE * y_size * capacity

    def project(j, carry):
        z = lax.rem(my_z + j, shards)
        for piece in range(2):
            share_copy(piece, z, 1 - core).wait_recv()
        weights = jnp.concatenate((first[2 * z], first[2 * z + 1]), axis=1)
        hidden = dot(expert_rows[...], weights)
        values, slopes = gelu_pair(hidden[:count], hidden[count:])
        cols = pl.ds(pl.multiple_of(z * 2 * units, 2 * units), 2 * units)
        active[:count, cols] = values.astype(BF16)
        active[count:, cols] = slopes.astype(BF16)
        return carry

    lax.fori_loop(0, shards, project, 0)
    block = y_size * capacity

    def h_copy(c, dest, slot):
        return pltpu.make_async_remote_copy(
            src_ref=halves_send.at[c, dest],
            dst_ref=halves.at[c, slot],
            send_sem=h_sent.at[c, dest],
            recv_sem=h_came.at[c, slot],
            device_id=at_x(dest),
            device_id_type=MESH,
        )

    def s_copy(c, dest, slot):
        return pltpu.make_async_remote_copy(
            src_ref=sums_send.at[c, dest],
            dst_ref=sums.at[c, slot],
            send_sem=s_sent.at[c, dest],
            recv_sem=s_came.at[c, slot],
            device_id=at_y(dest),
            device_id_type=MESH,
        )

    def expert_block(c):
        def arrive(z, carry):
            share_copy(2 + c, z, 1 - core).wait_recv()
            return carry

        lax.fori_loop(0, shards, arrive, 0)
        done = dot(active[...], second[:, c * CHUNK : (c + 1) * CHUNK]).astype(BF16)
        for x in range(X_SIZE):
            halves_send[c, x, :block] = done[x * block : (x + 1) * block]
            halves_send[c, x, block:] = done[count + x * block : count + (x + 1) * block]
        for j in (1, 3, 2):
            h_copy(c, lax.rem(my_x + j, X_SIZE), my_x).start()
        halves[c, my_x] = halves_send[c, my_x]

    def return_block(c):
        for j in (1, 3, 2):
            source = lax.rem(my_x + j, X_SIZE)
            h_copy(c, source, source).wait_recv()
        pair = [
            (halves[c, 2 * p].astype(F32) + halves[c, 2 * p + 1].astype(F32)).astype(BF16)
            for p in range(2)
        ]
        stacked = jnp.concatenate(
            [
                jnp.concatenate([total[:, i * 128 : (i + 1) * 128] for total in pair], axis=1)
                for i in range(parts)
            ],
            axis=0,
        )
        ready = dot(back_sort[...], stacked)
        for y in range(y_size):
            piece = ready[y * back_depth : (y + 1) * back_depth]
            sums_send[c, y] = jnp.concatenate((piece[:, :128], piece[:, 128:]), axis=0).astype(
                BF16
            )
        for j in order:
            s_copy(c, lax.rem(my_y + j, y_size), my_y).start()
        sums[c, my_y] = sums_send[c, my_y]

    def mix_block(c):
        for j in order:
            source = lax.rem(my_y + j, y_size)
            s_copy(c, source, source).wait_recv()
        values = sums[c].reshape(experts * back_depth, 128)
        mixed = (dot(gate_high[...], values) * 256.0 + dot(gate_low[...], values)) * (
            1.0 / 65536.0
        )
        for i in range(parts):
            cols = slice(c * CHUNK + i * 128, c * CHUNK + (i + 1) * 128)
            top = 2 * i * rows
            out[:, cols] = (state[:, cols] + mixed[top : top + rows]).astype(BF16)
            out_tangent[:, cols] = (
                tangent[:, cols] + mixed[top + rows : top + 2 * rows]
            ).astype(BF16)

    ring_step(2, 3)
    ring_step(3, 3)
    ring_step(4, 1)
    ring_step(5, 1)
    ring_step(2, 4)
    expert_block(0)
    ring_step(3, 4)
    ring_step(4, 2)
    ring_step(5, 2)
    expert_block(1)
    return_block(0)
    for hop in (3, 4):
        ring_step(4, hop)
        ring_step(5, hop)
    expert_block(2)
    return_block(1)
    expert_block(3)
    return_block(2)
    mix_block(0)
    return_block(3)
    for c in range(1, chunks):
        mix_block(c)

    def drain(j, carry):
        other = lax.rem(me + j, n)
        yz_copy(other, me).wait_send()
        x_copy(other, me).wait_send()
        o_copy(other, me).wait_send()
        return carry

    lax.fori_loop(1, n, drain, 0)

    def drain_shares(z, carry):
        for piece in range(RING_PIECES):
            share_copy(piece, z, core).wait_send()
        return carry

    lax.fori_loop(0, shards, drain_shares, 0)
    for piece in range(RING_PIECES):
        for way in range(2):
            for hop in range(1, hops(piece, way) + 1):
                ring_copy(piece, way, hop, False).wait_send()
    for j in order:
        m_copy(lax.rem(my_y + j, y_size), my_y).wait_send()
    for y in range(y_size):
        for j in range(1, X_SIZE):
            f_copy(lax.rem(my_x + j, X_SIZE), my_x, y).wait_send()
    for c in range(chunks):
        for j in range(1, X_SIZE):
            h_copy(c, lax.rem(my_x + j, X_SIZE), my_x).wait_send()
        for j in order:
            s_copy(c, lax.rem(my_y + j, y_size), my_y).wait_send()


def per_device(
    query_rows,
    key_rows,
    value_rows,
    query_tangent,
    key_tangent,
    value_tangent,
    stream,
    stream_tangent,
    norm_gain,
    expert_ids,
    gate_units,
    slot_index,
    weight_in,
    weight_out,
):
    n = lax.axis_size("seq")
    y_size = lax.axis_size("exp") // X_SIZE
    experts = 2 * y_size
    rows, width = stream.shape
    units = weight_out.shape[0]
    capacity = 2 * ((5 * rows + 4 * experts - 1) // (4 * experts))
    total = n * rows
    chunks = width // CHUNK
    depth = 2 * capacity * chunks
    parts = CHUNK // 128
    back_depth = parts * 2 * capacity
    block = y_size * capacity
    back_size = parts * 2 * block
    pair = 2 * HEAD_DIM
    vmem = pl.BlockSpec(memory_space=pltpu.VMEM)
    away = pl.BlockSpec(memory_space=pltpu.HBM)
    dma = pltpu.SemaphoreType.DMA

    def held(*shape):
        return pltpu.VMEM(shape, BF16)

    return pl.pallas_call(
        functools.partial(block_kernel, n, y_size, capacity),
        out_shape=(
            jax.ShapeDtypeStruct((rows, width), BF16),
            jax.ShapeDtypeStruct((rows, width), BF16),
        ),
        in_specs=[away] * 14,
        out_specs=(vmem,) * 2,
        scratch_shapes=[
            held(8, rows, width),
            pltpu.VMEM((1, width), F32),
            pltpu.VMEM((3, 2, rows), jnp.int32),
            held(n, width, units),
            held(n * units, width),
            held(n, rows, pair),
            held(n, rows, 2 * pair),
            held(total, pair),
            held(total, 2 * pair),
            held(pair, total),
            held(pair, total),
            held(total, pair),
            held(total, pair),
            held(n, rows, pair),
            held(experts * depth, 2 * chunks * rows),
            held(y_size // 2 * depth, y_size // 2 * depth),
            held(2 * chunks * rows, CHUNK),
            held(y_size, 2 * depth, CHUNK),
            held(y_size, 2 * depth, CHUNK),
            held(X_SIZE, y_size, depth, CHUNK),
            pltpu.VMEM((rows, width), F32),
            pltpu.VMEM((rows, width), F32),
            held(2 * X_SIZE * block, width),
            held(2 * X_SIZE * block, n * units),
            held(back_size, back_size),
            held(2 * parts * rows, experts * back_depth),
            held(2 * parts * rows, experts * back_depth),
            held(chunks, X_SIZE, 2 * block, CHUNK),
            held(chunks, X_SIZE, 2 * block, CHUNK),
            held(chunks, y_size, 2 * back_depth, 128),
            held(chunks, y_size, 2 * back_depth, 128),
        ]
        + [dma((14,))]
        + [dma((n,))] * 6
        + [dma((y_size,))] * 2
        + [dma((X_SIZE, y_size))] * 2
        + [dma((RING_PIECES, 2 * HOPS))] * 2
        + [dma((RING_PIECES, n // 2))] * 2
        + [dma((chunks, X_SIZE))] * 2
        + [dma((chunks, y_size))] * 2,
        compiler_params=pltpu.CompilerParams(
            collective_id=0, has_side_effects=True, vmem_limit_bytes=56 * 1024 * 1024
        ),
        name="moe_block",
    )(
        query_rows,
        key_rows,
        value_rows,
        query_tangent,
        key_tangent,
        value_tangent,
        stream,
        stream_tangent,
        norm_gain.reshape(1, width),
        expert_ids.T,
        gate_units.T,
        slot_index.T,
        weight_in,
        weight_out,
    )


def solution(mesh):
    rows = P(("exp", "seq"), None)
    return jax.shard_map(
        per_device,
        mesh=mesh,
        in_specs=(rows,) * 8 + (P(),) + (rows,) * 3 + (P(None, ("exp", "seq")), rows),
        out_specs=(rows, rows),
        check_vma=False,
    )
```

```python
import functools

import jax
import jax.numpy as jnp
from jax import lax
from jax.experimental import pallas as pl
from jax.experimental.pallas import tpu as pltpu
from jax.sharding import PartitionSpec as P

MESH = pl.DeviceIdType.MESH
HEAD_DIM = 64
BF16 = jnp.bfloat16
F32 = jnp.float32

epsilon = 1e-06
gelu_coef = 0.7978845608028654
cubic_coef = 0.044715


def gelu_pair(inputs, tangent):
    inner_arg = gelu_coef * (inputs + cubic_coef * inputs * inputs * inputs)
    hyperbolic = jnp.tanh(inner_arg)
    values = 0.5 * inputs * (1.0 + hyperbolic)
    slopes = 0.5 * (1.0 + hyperbolic) + 0.5 * inputs * (
        1.0 - hyperbolic * hyperbolic
    ) * gelu_coef * (1.0 + 3.0 * cubic_coef * inputs * inputs)
    return (values, slopes * tangent)


def dot(a, b):
    return jnp.dot(a, b, preferred_element_type=F32)


def one_hot(rows, columns):
    return jnp.where(rows == columns, 1.0, 0.0).astype(BF16)


def iota(shape, dim):
    return lax.broadcasted_iota(jnp.int32, shape, dim)


def ring_order(count):
    order = []
    for j in range(1, count // 2):
        order += [j, count - j]
    return order + [count // 2]


X_SIZE = 4
CHUNK = 256


ROUNDS = 1
RING_PIECES = 6
HOPS = 4


def block_kernel(
    n,
    y_size,
    capacity,
    q_in,
    k_in,
    v_in,
    dq_in,
    dk_in,
    dv_in,
    stream_in,
    stream_tangent_in,
    gain_in,
    ids_in,
    gates_in,
    slots_in,
    first_in,
    second_in,
    out,
    out_tangent,
    fetched,
    gain,
    numbers,
    first,
    second,
    x_send,
    yz_send,
    x_all,
    yz_all,
    k_top,
    k_low,
    z_low,
    o_send,
    o_all,
    pick,
    sort,
    tokens,
    message,
    middle,
    landed,
    state,
    tangent,
    expert_rows,
    active,
    back_sort,
    gate_high,
    gate_low,
    halves_send,
    halves,
    sums_send,
    sums,
    fetch_sem,
    x_sent,
    x_came,
    yz_sent,
    yz_came,
    o_sent,
    o_came,
    m_sent,
    m_came,
    f_sent,
    f_came,
    w_sent,
    w_came,
    p_sent,
    p_came,
    h_sent,
    h_came,
    s_sent,
    s_came,
):
    rows, width = stream_in.shape
    units = first_in.shape[1]
    me = lax.axis_index("seq")
    core = lax.rem(me, 2)
    partner = me + 1 - 2 * core
    my_z = me // 2
    shards = n // 2
    place = lax.axis_index("exp")
    my_x, my_y = lax.rem(place, X_SIZE), place // X_SIZE
    chunks = width // CHUNK
    experts = 2 * y_size
    span_codes = experts * capacity
    order = ring_order(y_size)

    def at_y(y):
        return {"exp": y * X_SIZE + my_x}

    def at_x(x):
        return {"exp": my_y * X_SIZE + x}

    def part(index):
        return pl.ds(pl.multiple_of(index * rows, rows), rows)

    def unit_rows(index):
        return pl.ds(pl.multiple_of(index * units, units), units)

    sources = (q_in, k_in, v_in, dq_in, dk_in, dv_in, stream_in, stream_tangent_in)
    targets = [fetched.at[i] for i in range(8)]
    sources += (gain_in, ids_in, gates_in, slots_in, first_in, second_in)
    targets += [gain, numbers.at[0], numbers.at[1], numbers.at[2]]
    targets += [first.at[me], second.at[unit_rows(me)]]
    fetches = [
        pltpu.make_async_copy(source, target, fetch_sem.at[i])
        for i, (source, target) in enumerate(zip(sources, targets))
    ]
    for copy in fetches:
        copy.start()

    barrier = pltpu.get_barrier_semaphore()

    def greet(j, carry):
        pl.semaphore_signal(
            barrier, inc=1, device_id={"seq": lax.rem(me + j, n)}, device_id_type=MESH
        )
        return carry

    lax.fori_loop(1, n, greet, 0)
    for j in range(1, y_size):
        pl.semaphore_signal(
            barrier, inc=1, device_id=at_y(lax.rem(my_y + j, y_size)), device_id_type=MESH
        )
    for j in range(1, X_SIZE):
        pl.semaphore_signal(
            barrier, inc=1, device_id=at_x(lax.rem(my_x + j, X_SIZE)), device_id_type=MESH
        )

    def piece_at(piece, index):
        if piece < 2:
            return first.at[index, piece * (width // 2) : (piece + 1) * (width // 2)]
        cols = slice((piece - 2) * CHUNK, (piece - 1) * CHUNK)
        return second.at[unit_rows(index), cols]

    def hops(piece, way):
        return HOPS if (piece + way) % 2 == 0 else HOPS - 1

    def ring_copy(piece, way, hop, arriving):
        step = 1 if way == 0 else shards - 1
        back = hop if arriving else hop - 1
        origin = lax.rem(my_z + (shards - step) * back, shards)
        block = piece_at(piece, 2 * origin + core)
        return pltpu.make_async_remote_copy(
            src_ref=block,
            dst_ref=block,
            send_sem=w_sent.at[piece, way * HOPS + hop - 1],
            recv_sem=w_came.at[piece, way * HOPS + hop - 1],
            device_id={"seq": 2 * lax.rem(my_z + step, shards) + core},
            device_id_type=MESH,
        )

    def share_copy(piece, z, owner):
        block = piece_at(piece, 2 * z + owner)
        return pltpu.make_async_remote_copy(
            src_ref=block,
            dst_ref=block,
            send_sem=p_sent.at[piece, z],
            recv_sem=p_came.at[piece, z],
            device_id={"seq": partner},
            device_id_type=MESH,
        )

    def ring_open(piece):
        for way in range(2):
            ring_copy(piece, way, 1, False).start()
        share_copy(piece, my_z, core).start()

    def ring_step(piece, hop):
        for way in range(2):
            if hop <= hops(piece, way):
                ring_copy(piece, way, hop, True).wait_recv()
                if hop < hops(piece, way):
                    ring_copy(piece, way, hop + 1, False).start()
                step = 1 if way == 0 else shards - 1
                origin = lax.rem(my_z + (shards - step) * hop, shards)
                share_copy(piece, origin, core).start()

    for copy in fetches[:6]:
        copy.wait()
    for h in range(n):
        cols = slice(h * HEAD_DIM, (h + 1) * HEAD_DIM)
        q, k, v, dq, dk, dv = (fetched[i, :, cols] for i in range(6))
        x_send[h] = jnp.concatenate((dq, q), axis=1) * BF16(HEAD_DIM**-0.5)
        yz_send[h] = jnp.concatenate((k, dk, v, dv), axis=1)
    pl.semaphore_wait(barrier, n - 1 + y_size - 1 + X_SIZE - 1)

    def yz_copy(dest, slot):
        return pltpu.make_async_remote_copy(
            src_ref=yz_send.at[dest],
            dst_ref=yz_all.at[part(slot)],
            send_sem=yz_sent.at[dest],
            recv_sem=yz_came.at[slot],
            device_id={"seq": dest},
            device_id_type=MESH,
        )

    def x_copy(dest, slot):
        return pltpu.make_async_remote_copy(
            src_ref=x_send.at[dest],
            dst_ref=x_all.at[part(slot)],
            send_sem=x_sent.at[dest],
            recv_sem=x_came.at[slot],
            device_id={"seq": dest},
            device_id_type=MESH,
        )

    def o_copy(dest, slot):
        return pltpu.make_async_remote_copy(
            src_ref=o_send.at[part(dest)],
            dst_ref=o_all.at[slot],
            send_sem=o_sent.at[dest],
            recv_sem=o_came.at[slot],
            device_id={"seq": dest},
            device_id_type=MESH,
        )

    for make in (yz_copy, x_copy):

        def send(j, carry):
            make(lax.rem(me + j, n), me).start()
            make(lax.rem(me + n - j, n), me).start()
            return carry

        lax.fori_loop(1, n // 2, send, 0)
        make(lax.rem(me + n // 2, n), me).start()

    yz_all[part(me)] = yz_send[me]
    x_all[part(me)] = x_send[me]
    for copy in fetches[6:]:
        copy.wait()

    codes = jnp.where(numbers[2] >= 0, numbers[0] * capacity + numbers[2], -1)
    wide = [
        jnp.concatenate(
            [jnp.where(row >= 0, row + span_codes * i, -1) for i in range(2 * chunks)], axis=1
        )
        for row in (codes[:1], codes[1:])
    ]
    depth = 2 * capacity * chunks
    line = iota((depth, 1), 0)
    wanted = lax.rem(line, capacity) + span_codes * (line // capacity)

    def choose(expert, carry):
        target = wanted + expert * capacity
        hit = (target == wide[0]) | (target == wide[1])
        pick[pl.ds(pl.multiple_of(expert * depth, depth), depth)] = jnp.where(
            hit, 1.0, 0.0
        ).astype(BF16)
        return carry

    lax.fori_loop(0, experts, choose, 0)
    half = y_size // 2
    size = half * depth
    line = iota((size, 1), 0)
    inner = lax.rem(line, half * capacity)
    sort[...] = one_hot(
        (inner // capacity) * depth
        + (line // (half * capacity)) * capacity
        + lax.rem(inner, capacity),
        iota((size, size), 1),
    )

    parts = CHUNK // 128
    back_depth = parts * 2 * capacity
    line = iota((1, experts * back_depth), 1)
    inner = lax.rem(line, back_depth)
    column_codes = (
        (line // back_depth) * capacity
        + lax.rem(inner, capacity)
        + span_codes * (inner // capacity)
    )

    def upright(row):
        return jnp.broadcast_to(row.astype(F32), (128, rows)).T[:, :1].astype(jnp.int32)

    high = jnp.zeros((2 * parts * rows, experts * back_depth), F32)
    low = high
    for choice in range(2):
        code = upright(codes[choice : choice + 1])
        gate = upright(numbers[1, choice : choice + 1])
        code = jnp.concatenate(
            [jnp.where(code >= 0, code + span_codes * i, -1) for i in range(2 * parts)], axis=0
        )
        top = gate // 256
        rest = gate - top * 256
        top = jnp.concatenate([top.astype(F32)] * (2 * parts), axis=0)
        rest = jnp.concatenate([rest.astype(F32)] * (2 * parts), axis=0)
        hit = code == column_codes
        high = high + jnp.where(hit, top, 0.0)
        low = low + jnp.where(hit, rest, 0.0)
    gate_high[...] = high.astype(BF16)
    gate_low[...] = low.astype(BF16)
    back_size = parts * 2 * y_size * capacity
    line = iota((back_size, 1), 0)
    inner = lax.rem(line, back_depth)
    back_sort[...] = one_hot(
        (inner // capacity) * (y_size * capacity)
        + (line // back_depth) * capacity
        + lax.rem(inner, capacity),
        iota((back_size, back_size), 1),
    )

    def yz_arrive(j, carry):
        other = lax.rem(me + j, n)
        yz_copy(other, other).wait_recv()
        return carry

    lax.fori_loop(1, n, yz_arrive, 0)
    ring_open(0)
    ring_open(1)
    turned = yz_all[:, : 2 * HEAD_DIM].T
    k_low[...] = turned
    k_top[:HEAD_DIM] = jnp.zeros_like(turned[:HEAD_DIM])
    k_top[HEAD_DIM:] = turned[:HEAD_DIM]
    z_low[...] = jnp.concatenate(
        (
            jnp.zeros((n * rows, HEAD_DIM), BF16),
            yz_all[:, 2 * HEAD_DIM : 3 * HEAD_DIM],
        ),
        axis=1,
    )
    per = 4
    blocks = n // per
    for i in range(blocks):
        block = lax.rem(me // per + i, blocks)
        for u in range(per):
            other = block * per + u

            @pl.when(other != me)
            def _():
                x_copy(other, other).wait_recv()

        span = pl.ds(pl.multiple_of(block * per * rows, per * rows), per * rows)
        x = x_all[span]
        scores = dot(x, k_top[...])
        drift = dot(x, k_low[...])
        weights = jnp.exp(scores - jnp.max(scores, axis=1, keepdims=True))
        weights = weights * (1.0 / jnp.sum(weights, axis=1, keepdims=True))
        drifted = weights * drift
        mean = jnp.sum(drifted, axis=1, keepdims=True)
        both = dot(weights.astype(BF16), yz_all[:, 2 * HEAD_DIM :])
        low = dot(drifted.astype(BF16), z_low[...])
        attended = both[:, :HEAD_DIM]
        moved = low[:, HEAD_DIM:] - mean * attended + both[:, HEAD_DIM:]
        o_send[span] = jnp.concatenate((attended, moved), axis=1).astype(BF16)
        for u in range(per):
            other = block * per + u

            @pl.when(other != me)
            def _():
                o_copy(other, me).start()

    o_all[me] = o_send[part(me)]
    ring_step(0, 1)
    ring_step(1, 1)
    ring_open(2)
    ring_open(3)

    def o_arrive(j, carry):
        other = lax.rem(me + j, n)
        o_copy(other, other).wait_recv()
        return carry

    lax.fori_loop(1, n, o_arrive, 0)
    for h in range(0, n, 2):
        cols = slice(h * HEAD_DIM, (h + 2) * HEAD_DIM)
        one = o_all[h].astype(F32)
        two = o_all[h + 1].astype(F32)
        state[:, cols] = fetched[6, :, cols].astype(F32) + jnp.concatenate(
            (one[:, :HEAD_DIM], two[:, :HEAD_DIM]), axis=1
        )
        tangent[:, cols] = fetched[7, :, cols].astype(F32) + jnp.concatenate(
            (one[:, HEAD_DIM:], two[:, HEAD_DIM:]), axis=1
        )
    wide_state = state[...]
    wide_tangent = tangent[...]
    inverse = lax.rsqrt(jnp.mean(wide_state * wide_state, axis=1, keepdims=True) + epsilon)
    cross = jnp.mean(wide_state * wide_tangent, axis=1, keepdims=True)
    normed = (gain[...] * wide_state * inverse).astype(BF16)
    normed_tangent = (
        gain[...] * inverse * (wide_tangent - wide_state * cross * inverse * inverse)
    ).astype(BF16)
    for c in range(chunks):
        cols = slice(c * CHUNK, (c + 1) * CHUNK)
        tokens[2 * c * rows : (2 * c + 1) * rows] = normed[:, cols]
        tokens[(2 * c + 1) * rows : (2 * c + 2) * rows] = normed_tangent[:, cols]

    def round_cols(turn):
        return slice(turn * (CHUNK // ROUNDS), (turn + 1) * (CHUNK // ROUNDS))

    def m_copy(dest, slot, turn):
        return pltpu.make_async_remote_copy(
            src_ref=message.at[dest, :, round_cols(turn)],
            dst_ref=middle.at[slot, :, round_cols(turn)],
            send_sem=m_sent.at[turn, dest],
            recv_sem=m_came.at[turn, slot],
            device_id=at_y(dest),
            device_id_type=MESH,
        )

    def f_copy(dest, source_x, source_y, turn):
        pair = pl.ds(pl.multiple_of((dest // 2) * depth, depth), depth)
        return pltpu.make_async_remote_copy(
            src_ref=middle.at[source_y, pair, round_cols(turn)],
            dst_ref=landed.at[source_x, source_y, :, round_cols(turn)],
            send_sem=f_sent.at[turn, dest, source_y],
            recv_sem=f_came.at[turn, source_x, source_y],
            device_id=at_x(dest),
            device_id_type=MESH,
        )

    def fill(dest):
        picked = pick[pl.ds(pl.multiple_of(dest * 2 * depth, 2 * depth), 2 * depth)]
        return dot(picked, tokens[...]).astype(BF16)

    def spread(source_y, turn):
        for j in (1, 3, 2):
            f_copy(lax.rem(my_x + j, X_SIZE), my_x, source_y, turn).start()

    for j in order:
        dest = lax.rem(my_y + j, y_size)
        message[dest] = fill(dest)
        m_copy(dest, my_y, 0).start()
    for turn in range(1, ROUNDS):
        for j in order:
            m_copy(lax.rem(my_y + j, y_size), my_y, turn).start()
    middle[my_y] = fill(my_y)
    for turn in range(ROUNDS):
        spread(my_y, turn)
    ring_step(0, 2)
    ring_step(1, 2)
    for turn in range(ROUNDS):
        for i, j in enumerate(order):
            other = lax.rem(my_y + j, y_size)
            m_copy(other, other, turn).wait_recv()
            spread(other, turn)
            if i == 1:
                ring_step(2, 1)
                ring_step(3, 1)
            if i == 3:
                ring_step(0, 3)
                ring_step(1, 3)
                ring_open(4)
                ring_open(5)
            if i == 5:
                ring_step(2, 2)
                ring_step(3, 2)
            if i == 6:
                ring_step(0, 4)
                ring_step(1, 4)
                ring_step(4, 1)
                ring_step(5, 1)
    own_pair = pl.ds(pl.multiple_of((my_x // 2) * depth, depth), depth)
    for y in range(y_size):
        landed[my_x, y] = middle[y, own_pair]
    for j in [0] + order:
        other = lax.rem(my_y + j, y_size)
        for i in range(1, X_SIZE):
            source = lax.rem(my_x + i, X_SIZE)
            for turn in range(ROUNDS):
                f_copy(source, source, other, turn).wait_recv()
    group = half * capacity
    for x in range(X_SIZE):
        sorted_rows = [
            dot(sort[...], landed[x, side * half : (side + 1) * half].reshape(size, CHUNK))
            for side in range(2)
        ]
        for c in range(chunks):
            for kind in range(2):
                top = (2 * c + kind) * group
                expert_rows[
                    pl.ds((kind * X_SIZE + x) * 2 * group, 2 * group),
                    pl.ds(c * CHUNK, CHUNK),
                ] = jnp.concatenate(
                    [values[top : top + group] for values in sorted_rows], axis=0
                ).astype(BF16)
    ring_step(2, 3)
    ring_step(3, 3)
    ring_step(4, 2)
    ring_step(5, 2)

    count = X_SIZE * y_size * capacity

    def project(j, carry):
        z = lax.rem(my_z + j, shards)
        for piece in range(2):
            share_copy(piece, z, 1 - core).wait_recv()
        weights = jnp.concatenate((first[2 * z], first[2 * z + 1]), axis=1)
        hidden = dot(expert_rows[...], weights)
        values, slopes = gelu_pair(hidden[:count], hidden[count:])
        cols = pl.ds(pl.multiple_of(z * 2 * units, 2 * units), 2 * units)
        active[:count, cols] = values.astype(BF16)
        active[count:, cols] = slopes.astype(BF16)
        return carry

    lax.fori_loop(0, shards // 2, project, 0)
    ring_step(2, 4)
    ring_step(3, 4)
    ring_step(4, 3)
    ring_step(5, 3)
    lax.fori_loop(shards // 2, shards, project, 0)
    block = y_size * capacity

    def h_copy(c, dest, slot):
        return pltpu.make_async_remote_copy(
            src_ref=halves_send.at[c, dest],
            dst_ref=halves.at[c, slot],
            send_sem=h_sent.at[c, dest],
            recv_sem=h_came.at[c, slot],
            device_id=at_x(dest),
            device_id_type=MESH,
        )

    def s_copy(c, dest, slot):
        return pltpu.make_async_remote_copy(
            src_ref=sums_send.at[c, dest],
            dst_ref=sums.at[c, slot],
            send_sem=s_sent.at[c, dest],
            recv_sem=s_came.at[c, slot],
            device_id=at_y(dest),
            device_id_type=MESH,
        )

    def expert_block(c):
        def arrive(z, carry):
            share_copy(2 + c, z, 1 - core).wait_recv()
            return carry

        lax.fori_loop(0, shards, arrive, 0)
        done = dot(active[...], second[:, c * CHUNK : (c + 1) * CHUNK]).astype(BF16)
        for x in range(X_SIZE):
            halves_send[c, x, :block] = done[x * block : (x + 1) * block]
            halves_send[c, x, block:] = done[count + x * block : count + (x + 1) * block]
        for j in (1, 3, 2):
            h_copy(c, lax.rem(my_x + j, X_SIZE), my_x).start()
        halves[c, my_x] = halves_send[c, my_x]

    def return_block(c):
        for j in (1, 3, 2):
            source = lax.rem(my_x + j, X_SIZE)
            h_copy(c, source, source).wait_recv()
        pair = [
            (halves[c, 2 * p].astype(F32) + halves[c, 2 * p + 1].astype(F32)).astype(BF16)
            for p in range(2)
        ]
        stacked = jnp.concatenate(
            [
                jnp.concatenate([total[:, i * 128 : (i + 1) * 128] for total in pair], axis=1)
                for i in range(parts)
            ],
            axis=0,
        )
        ready = dot(back_sort[...], stacked)
        for y in range(y_size):
            piece = ready[y * back_depth : (y + 1) * back_depth]
            sums_send[c, y] = jnp.concatenate((piece[:, :128], piece[:, 128:]), axis=0).astype(
                BF16
            )
        for j in order:
            s_copy(c, lax.rem(my_y + j, y_size), my_y).start()
        sums[c, my_y] = sums_send[c, my_y]

    def mix_block(c):
        for j in order:
            source = lax.rem(my_y + j, y_size)
            s_copy(c, source, source).wait_recv()
        values = sums[c].reshape(experts * back_depth, 128)
        mixed = (dot(gate_high[...], values) * 256.0 + dot(gate_low[...], values)) * (
            1.0 / 65536.0
        )
        for i in range(parts):
            cols = slice(c * CHUNK + i * 128, c * CHUNK + (i + 1) * 128)
            top = 2 * i * rows
            out[:, cols] = state[:, cols] + mixed[top : top + rows]
            out_tangent[:, cols] = tangent[:, cols] + mixed[top + rows : top + 2 * rows]

    ring_step(4, 4)
    expert_block(0)
    expert_block(1)
    return_block(0)
    ring_step(5, 4)
    expert_block(2)
    return_block(1)
    expert_block(3)
    return_block(2)
    mix_block(0)
    return_block(3)
    for c in range(1, chunks):
        mix_block(c)

    def drain(j, carry):
        other = lax.rem(me + j, n)
        yz_copy(other, me).wait_send()
        x_copy(other, me).wait_send()
        o_copy(other, me).wait_send()
        return carry

    lax.fori_loop(1, n, drain, 0)

    def drain_shares(z, carry):
        for piece in range(RING_PIECES):
            share_copy(piece, z, core).wait_send()
        return carry

    lax.fori_loop(0, shards, drain_shares, 0)
    for piece in range(RING_PIECES):
        for way in range(2):
            for hop in range(1, hops(piece, way) + 1):
                ring_copy(piece, way, hop, False).wait_send()
    for j in order:
        for turn in range(ROUNDS):
            m_copy(lax.rem(my_y + j, y_size), my_y, turn).wait_send()
    for y in range(y_size):
        for j in range(1, X_SIZE):
            for turn in range(ROUNDS):
                f_copy(lax.rem(my_x + j, X_SIZE), my_x, y, turn).wait_send()
    for c in range(chunks):
        for j in range(1, X_SIZE):
            h_copy(c, lax.rem(my_x + j, X_SIZE), my_x).wait_send()
        for j in order:
            s_copy(c, lax.rem(my_y + j, y_size), my_y).wait_send()


def per_device(
    query_rows,
    key_rows,
    value_rows,
    query_tangent,
    key_tangent,
    value_tangent,
    stream,
    stream_tangent,
    norm_gain,
    expert_ids,
    gate_units,
    slot_index,
    weight_in,
    weight_out,
):
    n = lax.axis_size("seq")
    y_size = lax.axis_size("exp") // X_SIZE
    experts = 2 * y_size
    rows, width = stream.shape
    units = weight_out.shape[0]
    capacity = 2 * ((5 * rows + 4 * experts - 1) // (4 * experts))
    total = n * rows
    chunks = width // CHUNK
    depth = 2 * capacity * chunks
    parts = CHUNK // 128
    back_depth = parts * 2 * capacity
    block = y_size * capacity
    back_size = parts * 2 * block
    pair = 2 * HEAD_DIM
    vmem = pl.BlockSpec(memory_space=pltpu.VMEM)
    away = pl.BlockSpec(memory_space=pltpu.HBM)
    dma = pltpu.SemaphoreType.DMA

    def held(*shape):
        return pltpu.VMEM(shape, BF16)

    block_out, block_tangent = pl.pallas_call(
        functools.partial(block_kernel, n, y_size, capacity),
        out_shape=(
            jax.ShapeDtypeStruct((rows, width), F32),
            jax.ShapeDtypeStruct((rows, width), F32),
        ),
        in_specs=[away] * 14,
        out_specs=(vmem,) * 2,
        scratch_shapes=[
            held(8, rows, width),
            pltpu.VMEM((1, width), F32),
            pltpu.VMEM((3, 2, rows), jnp.int32),
            held(n, width, units),
            held(n * units, width),
            held(n, rows, pair),
            held(n, rows, 2 * pair),
            held(total, pair),
            held(total, 2 * pair),
            held(pair, total),
            held(pair, total),
            held(total, pair),
            held(total, pair),
            held(n, rows, pair),
            held(experts * depth, 2 * chunks * rows),
            held(y_size // 2 * depth, y_size // 2 * depth),
            held(2 * chunks * rows, CHUNK),
            held(y_size, 2 * depth, CHUNK),
            held(y_size, 2 * depth, CHUNK),
            held(X_SIZE, y_size, depth, CHUNK),
            pltpu.VMEM((rows, width), F32),
            pltpu.VMEM((rows, width), F32),
            held(2 * X_SIZE * block, width),
            held(2 * X_SIZE * block, n * units),
            held(back_size, back_size),
            held(2 * parts * rows, experts * back_depth),
            held(2 * parts * rows, experts * back_depth),
            held(chunks, X_SIZE, 2 * block, CHUNK),
            held(chunks, X_SIZE, 2 * block, CHUNK),
            held(chunks, y_size, 2 * back_depth, 128),
            held(chunks, y_size, 2 * back_depth, 128),
        ]
        + [dma((14,))]
        + [dma((n,))] * 6
        + [dma((ROUNDS, y_size))] * 2
        + [dma((ROUNDS, X_SIZE, y_size))] * 2
        + [dma((RING_PIECES, 2 * HOPS))] * 2
        + [dma((RING_PIECES, n // 2))] * 2
        + [dma((chunks, X_SIZE))] * 2
        + [dma((chunks, y_size))] * 2,
        compiler_params=pltpu.CompilerParams(
            collective_id=0, has_side_effects=True, vmem_limit_bytes=56 * 1024 * 1024
        ),
        name="moe_block",
    )(
        query_rows,
        key_rows,
        value_rows,
        query_tangent,
        key_tangent,
        value_tangent,
        stream,
        stream_tangent,
        norm_gain.reshape(1, width),
        expert_ids.T,
        gate_units.T,
        slot_index.T,
        weight_in,
        weight_out,
    )
    return block_out.astype(BF16), block_tangent.astype(BF16)


def solution(mesh):
    rows = P(("exp", "seq"), None)
    return jax.shard_map(
        per_device,
        mesh=mesh,
        in_specs=(rows,) * 8 + (P(),) + (rows,) * 3 + (P(None, ("exp", "seq")), rows),
        out_specs=(rows, rows),
        check_vma=False,
    )
```

```python
import functools

import jax
import jax.numpy as jnp
from jax import lax
from jax.experimental import pallas as pl
from jax.experimental.pallas import tpu as pltpu
from jax.sharding import PartitionSpec as P

MESH = pl.DeviceIdType.MESH
HEAD_DIM = 64
BF16 = jnp.bfloat16
F32 = jnp.float32

epsilon = 1e-06
gelu_coef = 0.7978845608028654
cubic_coef = 0.044715


def gelu_pair(inputs, tangent):
    inner_arg = gelu_coef * (inputs + cubic_coef * inputs * inputs * inputs)
    hyperbolic = jnp.tanh(inner_arg)
    values = 0.5 * inputs * (1.0 + hyperbolic)
    slopes = 0.5 * (1.0 + hyperbolic) + 0.5 * inputs * (
        1.0 - hyperbolic * hyperbolic
    ) * gelu_coef * (1.0 + 3.0 * cubic_coef * inputs * inputs)
    return (values, slopes * tangent)


def dot(a, b):
    return jnp.dot(a, b, preferred_element_type=F32)


def one_hot(rows, columns):
    return jnp.where(rows == columns, 1.0, 0.0).astype(BF16)


def iota(shape, dim):
    return lax.broadcasted_iota(jnp.int32, shape, dim)


def ring_order(count):
    order = []
    for j in range(1, count // 2):
        order += [j, count - j]
    return order + [count // 2]


X_SIZE = 4
CHUNK = 256


ROUNDS = 1
RING_PIECES = 6
HOPS = 4


def block_kernel(
    n,
    y_size,
    capacity,
    q_in,
    k_in,
    v_in,
    dq_in,
    dk_in,
    dv_in,
    stream_in,
    stream_tangent_in,
    gain_in,
    ids_in,
    gates_in,
    slots_in,
    first_in,
    second_in,
    both_out,
    fetched,
    gain,
    numbers,
    first,
    second,
    x_send,
    yz_send,
    x_all,
    yz_all,
    k_top,
    k_low,
    z_low,
    o_send,
    o_all,
    pick,
    sort,
    tokens,
    message,
    middle,
    landed,
    state,
    tangent,
    expert_rows,
    active,
    back_sort,
    gate_high,
    gate_low,
    halves_send,
    halves,
    sums_send,
    sums,
    fetch_sem,
    x_sent,
    x_came,
    yz_sent,
    yz_came,
    o_sent,
    o_came,
    m_sent,
    m_came,
    f_sent,
    f_came,
    w_sent,
    w_came,
    p_sent,
    p_came,
    h_sent,
    h_came,
    s_sent,
    s_came,
):
    rows, width = stream_in.shape
    units = first_in.shape[1]
    me = lax.axis_index("seq")
    core = lax.rem(me, 2)
    partner = me + 1 - 2 * core
    my_z = me // 2
    shards = n // 2
    place = lax.axis_index("exp")
    my_x, my_y = lax.rem(place, X_SIZE), place // X_SIZE
    chunks = width // CHUNK
    experts = 2 * y_size
    span_codes = experts * capacity
    order = ring_order(y_size)

    def at_y(y):
        return {"exp": y * X_SIZE + my_x}

    def at_x(x):
        return {"exp": my_y * X_SIZE + x}

    def part(index):
        return pl.ds(pl.multiple_of(index * rows, rows), rows)

    def unit_rows(index):
        return pl.ds(pl.multiple_of(index * units, units), units)

    sources = (q_in, k_in, v_in, dq_in, dk_in, dv_in, stream_in, stream_tangent_in)
    targets = [fetched.at[i] for i in range(8)]
    sources += (gain_in, ids_in, gates_in, slots_in, first_in, second_in)
    targets += [gain, numbers.at[0], numbers.at[1], numbers.at[2]]
    targets += [first.at[me], second.at[unit_rows(me)]]
    fetches = [
        pltpu.make_async_copy(source, target, fetch_sem.at[i])
        for i, (source, target) in enumerate(zip(sources, targets))
    ]
    for copy in fetches:
        copy.start()

    barrier = pltpu.get_barrier_semaphore()

    def greet(j, carry):
        pl.semaphore_signal(
            barrier, inc=1, device_id={"seq": lax.rem(me + j, n)}, device_id_type=MESH
        )
        return carry

    lax.fori_loop(1, n, greet, 0)
    for j in range(1, y_size):
        pl.semaphore_signal(
            barrier, inc=1, device_id=at_y(lax.rem(my_y + j, y_size)), device_id_type=MESH
        )
    for j in range(1, X_SIZE):
        pl.semaphore_signal(
            barrier, inc=1, device_id=at_x(lax.rem(my_x + j, X_SIZE)), device_id_type=MESH
        )

    def piece_at(piece, index):
        if piece < 2:
            return first.at[index, piece * (width // 2) : (piece + 1) * (width // 2)]
        cols = slice((piece - 2) * CHUNK, (piece - 1) * CHUNK)
        return second.at[unit_rows(index), cols]

    def hops(piece, way):
        return HOPS if (piece + way) % 2 == 0 else HOPS - 1

    def ring_copy(piece, way, hop, arriving):
        step = 1 if way == 0 else shards - 1
        back = hop if arriving else hop - 1
        origin = lax.rem(my_z + (shards - step) * back, shards)
        block = piece_at(piece, 2 * origin + core)
        return pltpu.make_async_remote_copy(
            src_ref=block,
            dst_ref=block,
            send_sem=w_sent.at[piece, way * HOPS + hop - 1],
            recv_sem=w_came.at[piece, way * HOPS + hop - 1],
            device_id={"seq": 2 * lax.rem(my_z + step, shards) + core},
            device_id_type=MESH,
        )

    def share_copy(piece, z, owner):
        block = piece_at(piece, 2 * z + owner)
        return pltpu.make_async_remote_copy(
            src_ref=block,
            dst_ref=block,
            send_sem=p_sent.at[piece, z],
            recv_sem=p_came.at[piece, z],
            device_id={"seq": partner},
            device_id_type=MESH,
        )

    def ring_open(piece):
        for way in range(2):
            ring_copy(piece, way, 1, False).start()
        share_copy(piece, my_z, core).start()

    def ring_step(piece, hop):
        for way in range(2):
            if hop <= hops(piece, way):
                ring_copy(piece, way, hop, True).wait_recv()
                if hop < hops(piece, way):
                    ring_copy(piece, way, hop + 1, False).start()
                step = 1 if way == 0 else shards - 1
                origin = lax.rem(my_z + (shards - step) * hop, shards)
                share_copy(piece, origin, core).start()

    for copy in fetches[:6]:
        copy.wait()
    for h in range(n):
        cols = slice(h * HEAD_DIM, (h + 1) * HEAD_DIM)
        q, k, v, dq, dk, dv = (fetched[i, :, cols] for i in range(6))
        x_send[h] = jnp.concatenate((dq, q), axis=1) * BF16(HEAD_DIM**-0.5)
        yz_send[h] = jnp.concatenate((k, dk, v, dv), axis=1)
    pl.semaphore_wait(barrier, n - 1 + y_size - 1 + X_SIZE - 1)

    def yz_copy(dest, slot):
        return pltpu.make_async_remote_copy(
            src_ref=yz_send.at[dest],
            dst_ref=yz_all.at[part(slot)],
            send_sem=yz_sent.at[dest],
            recv_sem=yz_came.at[slot],
            device_id={"seq": dest},
            device_id_type=MESH,
        )

    def x_copy(dest, slot):
        return pltpu.make_async_remote_copy(
            src_ref=x_send.at[dest],
            dst_ref=x_all.at[part(slot)],
            send_sem=x_sent.at[dest],
            recv_sem=x_came.at[slot],
            device_id={"seq": dest},
            device_id_type=MESH,
        )

    def o_copy(dest, slot):
        return pltpu.make_async_remote_copy(
            src_ref=o_send.at[part(dest)],
            dst_ref=o_all.at[slot],
            send_sem=o_sent.at[dest],
            recv_sem=o_came.at[slot],
            device_id={"seq": dest},
            device_id_type=MESH,
        )

    for make in (yz_copy, x_copy):

        def send(j, carry):
            make(lax.rem(me + j, n), me).start()
            make(lax.rem(me + n - j, n), me).start()
            return carry

        lax.fori_loop(1, n // 2, send, 0)
        make(lax.rem(me + n // 2, n), me).start()

    yz_all[part(me)] = yz_send[me]
    x_all[part(me)] = x_send[me]
    for copy in fetches[6:]:
        copy.wait()

    codes = jnp.where(numbers[2] >= 0, numbers[0] * capacity + numbers[2], -1)
    wide = [
        jnp.concatenate(
            [jnp.where(row >= 0, row + span_codes * i, -1) for i in range(2 * chunks)], axis=1
        )
        for row in (codes[:1], codes[1:])
    ]
    depth = 2 * capacity * chunks
    line = iota((depth, 1), 0)
    wanted = lax.rem(line, capacity) + span_codes * (line // capacity)

    def choose(expert, carry):
        target = wanted + expert * capacity
        hit = (target == wide[0]) | (target == wide[1])
        pick[pl.ds(pl.multiple_of(expert * depth, depth), depth)] = jnp.where(
            hit, 1.0, 0.0
        ).astype(BF16)
        return carry

    lax.fori_loop(0, experts, choose, 0)
    half = y_size // 2
    size = half * depth
    line = iota((size, 1), 0)
    inner = lax.rem(line, half * capacity)
    sort[...] = one_hot(
        (inner // capacity) * depth
        + (line // (half * capacity)) * capacity
        + lax.rem(inner, capacity),
        iota((size, size), 1),
    )

    parts = CHUNK // 128
    back_depth = parts * 2 * capacity
    line = iota((1, experts * back_depth), 1)
    inner = lax.rem(line, back_depth)
    column_codes = (
        (line // back_depth) * capacity
        + lax.rem(inner, capacity)
        + span_codes * (inner // capacity)
    )

    def upright(row):
        return jnp.broadcast_to(row.astype(F32), (128, rows)).T[:, :1].astype(jnp.int32)

    high = jnp.zeros((2 * parts * rows, experts * back_depth), F32)
    low = high
    for choice in range(2):
        code = upright(codes[choice : choice + 1])
        gate = upright(numbers[1, choice : choice + 1])
        code = jnp.concatenate(
            [jnp.where(code >= 0, code + span_codes * i, -1) for i in range(2 * parts)], axis=0
        )
        top = gate // 256
        rest = gate - top * 256
        top = jnp.concatenate([top.astype(F32)] * (2 * parts), axis=0)
        rest = jnp.concatenate([rest.astype(F32)] * (2 * parts), axis=0)
        hit = code == column_codes
        high = high + jnp.where(hit, top, 0.0)
        low = low + jnp.where(hit, rest, 0.0)
    gate_high[...] = high.astype(BF16)
    gate_low[...] = low.astype(BF16)
    back_size = parts * 2 * y_size * capacity
    line = iota((back_size, 1), 0)
    inner = lax.rem(line, back_depth)
    back_sort[...] = one_hot(
        (inner // capacity) * (y_size * capacity)
        + (line // back_depth) * capacity
        + lax.rem(inner, capacity),
        iota((back_size, back_size), 1),
    )

    def yz_arrive(j, carry):
        other = lax.rem(me + j, n)
        yz_copy(other, other).wait_recv()
        return carry

    lax.fori_loop(1, n, yz_arrive, 0)
    ring_open(0)
    ring_open(1)
    turned = yz_all[:, : 2 * HEAD_DIM].T
    k_low[...] = turned
    k_top[:HEAD_DIM] = jnp.zeros_like(turned[:HEAD_DIM])
    k_top[HEAD_DIM:] = turned[:HEAD_DIM]
    z_low[...] = jnp.concatenate(
        (
            jnp.zeros((n * rows, HEAD_DIM), BF16),
            yz_all[:, 2 * HEAD_DIM : 3 * HEAD_DIM],
        ),
        axis=1,
    )
    per = 4
    blocks = n // per
    for i in range(blocks):
        block = lax.rem(me // per + i, blocks)
        for u in range(per):
            other = block * per + u

            @pl.when(other != me)
            def _():
                x_copy(other, other).wait_recv()

        span = pl.ds(pl.multiple_of(block * per * rows, per * rows), per * rows)
        x = x_all[span]
        scores = dot(x, k_top[...])
        drift = dot(x, k_low[...])
        weights = jnp.exp(scores - jnp.max(scores, axis=1, keepdims=True))
        weights = weights * (1.0 / jnp.sum(weights, axis=1, keepdims=True))
        drifted = weights * drift
        mean = jnp.sum(drifted, axis=1, keepdims=True)
        both = dot(weights.astype(BF16), yz_all[:, 2 * HEAD_DIM :])
        low = dot(drifted.astype(BF16), z_low[...])
        attended = both[:, :HEAD_DIM]
        moved = low[:, HEAD_DIM:] - mean * attended + both[:, HEAD_DIM:]
        o_send[span] = jnp.concatenate((attended, moved), axis=1).astype(BF16)
        for u in range(per):
            other = block * per + u

            @pl.when(other != me)
            def _():
                o_copy(other, me).start()

    o_all[me] = o_send[part(me)]
    ring_step(0, 1)
    ring_step(1, 1)
    ring_open(2)
    ring_open(3)

    def o_arrive(j, carry):
        other = lax.rem(me + j, n)
        o_copy(other, other).wait_recv()
        return carry

    lax.fori_loop(1, n, o_arrive, 0)
    for h in range(0, n, 2):
        cols = slice(h * HEAD_DIM, (h + 2) * HEAD_DIM)
        one = o_all[h].astype(F32)
        two = o_all[h + 1].astype(F32)
        state[:, cols] = fetched[6, :, cols].astype(F32) + jnp.concatenate(
            (one[:, :HEAD_DIM], two[:, :HEAD_DIM]), axis=1
        )
        tangent[:, cols] = fetched[7, :, cols].astype(F32) + jnp.concatenate(
            (one[:, HEAD_DIM:], two[:, HEAD_DIM:]), axis=1
        )
    wide_state = state[...]
    wide_tangent = tangent[...]
    inverse = lax.rsqrt(jnp.mean(wide_state * wide_state, axis=1, keepdims=True) + epsilon)
    cross = jnp.mean(wide_state * wide_tangent, axis=1, keepdims=True)
    normed = (gain[...] * wide_state * inverse).astype(BF16)
    normed_tangent = (
        gain[...] * inverse * (wide_tangent - wide_state * cross * inverse * inverse)
    ).astype(BF16)
    for c in range(chunks):
        cols = slice(c * CHUNK, (c + 1) * CHUNK)
        tokens[2 * c * rows : (2 * c + 1) * rows] = normed[:, cols]
        tokens[(2 * c + 1) * rows : (2 * c + 2) * rows] = normed_tangent[:, cols]

    def round_cols(turn):
        return slice(turn * (CHUNK // ROUNDS), (turn + 1) * (CHUNK // ROUNDS))

    def m_copy(dest, slot, turn):
        return pltpu.make_async_remote_copy(
            src_ref=message.at[dest, :, round_cols(turn)],
            dst_ref=middle.at[slot, :, round_cols(turn)],
            send_sem=m_sent.at[turn, dest],
            recv_sem=m_came.at[turn, slot],
            device_id=at_y(dest),
            device_id_type=MESH,
        )

    def f_copy(dest, source_x, source_y, turn):
        pair = pl.ds(pl.multiple_of((dest // 2) * depth, depth), depth)
        return pltpu.make_async_remote_copy(
            src_ref=middle.at[source_y, pair, round_cols(turn)],
            dst_ref=landed.at[source_x, source_y, :, round_cols(turn)],
            send_sem=f_sent.at[turn, dest, source_y],
            recv_sem=f_came.at[turn, source_x, source_y],
            device_id=at_x(dest),
            device_id_type=MESH,
        )

    def fill(dest):
        picked = pick[pl.ds(pl.multiple_of(dest * 2 * depth, 2 * depth), 2 * depth)]
        return dot(picked, tokens[...]).astype(BF16)

    def spread(source_y, turn):
        for j in (1, 3, 2):
            f_copy(lax.rem(my_x + j, X_SIZE), my_x, source_y, turn).start()

    for j in order:
        dest = lax.rem(my_y + j, y_size)
        message[dest] = fill(dest)
        m_copy(dest, my_y, 0).start()
    for turn in range(1, ROUNDS):
        for j in order:
            m_copy(lax.rem(my_y + j, y_size), my_y, turn).start()
    middle[my_y] = fill(my_y)
    for turn in range(ROUNDS):
        spread(my_y, turn)
    ring_step(0, 2)
    ring_step(1, 2)
    for turn in range(ROUNDS):
        for i, j in enumerate(order):
            other = lax.rem(my_y + j, y_size)
            m_copy(other, other, turn).wait_recv()
            spread(other, turn)
            if i == 1:
                ring_step(2, 1)
                ring_step(3, 1)
            if i == 3:
                ring_step(0, 3)
                ring_step(1, 3)
                ring_open(4)
                ring_open(5)
            if i == 5:
                ring_step(2, 2)
                ring_step(3, 2)
            if i == 6:
                ring_step(0, 4)
                ring_step(1, 4)
                ring_step(4, 1)
                ring_step(5, 1)
    own_pair = pl.ds(pl.multiple_of((my_x // 2) * depth, depth), depth)
    for y in range(y_size):
        landed[my_x, y] = middle[y, own_pair]
    for j in [0] + order:
        other = lax.rem(my_y + j, y_size)
        for i in range(1, X_SIZE):
            source = lax.rem(my_x + i, X_SIZE)
            for turn in range(ROUNDS):
                f_copy(source, source, other, turn).wait_recv()
    group = half * capacity
    for x in range(X_SIZE):
        sorted_rows = [
            dot(sort[...], landed[x, side * half : (side + 1) * half].reshape(size, CHUNK))
            for side in range(2)
        ]
        for c in range(chunks):
            for kind in range(2):
                top = (2 * c + kind) * group
                expert_rows[
                    pl.ds((kind * X_SIZE + x) * 2 * group, 2 * group),
                    pl.ds(c * CHUNK, CHUNK),
                ] = jnp.concatenate(
                    [values[top : top + group] for values in sorted_rows], axis=0
                ).astype(BF16)
    ring_step(2, 3)
    ring_step(3, 3)
    ring_step(4, 2)
    ring_step(5, 2)

    count = X_SIZE * y_size * capacity

    def project(j, carry):
        z = lax.rem(my_z + j, shards)
        for piece in range(2):
            share_copy(piece, z, 1 - core).wait_recv()
        weights = jnp.concatenate((first[2 * z], first[2 * z + 1]), axis=1)
        hidden = dot(expert_rows[...], weights)
        values, slopes = gelu_pair(hidden[:count], hidden[count:])
        cols = pl.ds(pl.multiple_of(z * 2 * units, 2 * units), 2 * units)
        active[:count, cols] = values.astype(BF16)
        active[count:, cols] = slopes.astype(BF16)
        return carry

    lax.fori_loop(0, shards // 2, project, 0)
    ring_step(2, 4)
    ring_step(3, 4)
    ring_step(4, 3)
    ring_step(5, 3)
    lax.fori_loop(shards // 2, shards, project, 0)
    block = y_size * capacity

    def h_copy(c, dest, slot):
        return pltpu.make_async_remote_copy(
            src_ref=halves_send.at[c, dest],
            dst_ref=halves.at[c, slot],
            send_sem=h_sent.at[c, dest],
            recv_sem=h_came.at[c, slot],
            device_id=at_x(dest),
            device_id_type=MESH,
        )

    def s_copy(c, dest, slot):
        return pltpu.make_async_remote_copy(
            src_ref=sums_send.at[c, dest],
            dst_ref=sums.at[c, slot],
            send_sem=s_sent.at[c, dest],
            recv_sem=s_came.at[c, slot],
            device_id=at_y(dest),
            device_id_type=MESH,
        )

    def expert_block(c):
        def arrive(z, carry):
            share_copy(2 + c, z, 1 - core).wait_recv()
            return carry

        lax.fori_loop(0, shards, arrive, 0)
        done = dot(active[...], second[:, c * CHUNK : (c + 1) * CHUNK]).astype(BF16)
        for x in range(X_SIZE):
            halves_send[c, x, :block] = done[x * block : (x + 1) * block]
            halves_send[c, x, block:] = done[count + x * block : count + (x + 1) * block]
        for j in (1, 3, 2):
            h_copy(c, lax.rem(my_x + j, X_SIZE), my_x).start()
        halves[c, my_x] = halves_send[c, my_x]

    def return_block(c):
        for j in (1, 3, 2):
            source = lax.rem(my_x + j, X_SIZE)
            h_copy(c, source, source).wait_recv()
        pair = [
            (halves[c, 2 * p].astype(F32) + halves[c, 2 * p + 1].astype(F32)).astype(BF16)
            for p in range(2)
        ]
        stacked = jnp.concatenate(
            [
                jnp.concatenate([total[:, i * 128 : (i + 1) * 128] for total in pair], axis=1)
                for i in range(parts)
            ],
            axis=0,
        )
        ready = dot(back_sort[...], stacked)
        for y in range(y_size):
            piece = ready[y * back_depth : (y + 1) * back_depth]
            sums_send[c, y] = jnp.concatenate((piece[:, :128], piece[:, 128:]), axis=0).astype(
                BF16
            )
        for j in order:
            s_copy(c, lax.rem(my_y + j, y_size), my_y).start()
        sums[c, my_y] = sums_send[c, my_y]

    def mix_block(c):
        for j in order:
            source = lax.rem(my_y + j, y_size)
            s_copy(c, source, source).wait_recv()
        values = sums[c].reshape(experts * back_depth, 128)
        mixed = (dot(gate_high[...], values) * 256.0 + dot(gate_low[...], values)) * (
            1.0 / 65536.0
        )
        for i in range(parts):
            cols = slice(c * CHUNK + i * 128, c * CHUNK + (i + 1) * 128)
            top = 2 * i * rows
            both_out[:rows, cols] = (state[:, cols] + mixed[top : top + rows]).astype(BF16)
            both_out[rows:, cols] = (
                tangent[:, cols] + mixed[top + rows : top + 2 * rows]
            ).astype(BF16)

    ring_step(4, 4)
    expert_block(0)
    expert_block(1)
    return_block(0)
    ring_step(5, 4)
    expert_block(2)
    return_block(1)
    expert_block(3)
    return_block(2)
    mix_block(0)
    return_block(3)
    for c in range(1, chunks):
        mix_block(c)

    def drain(j, carry):
        other = lax.rem(me + j, n)
        yz_copy(other, me).wait_send()
        x_copy(other, me).wait_send()
        o_copy(other, me).wait_send()
        return carry

    lax.fori_loop(1, n, drain, 0)

    def drain_shares(z, carry):
        for piece in range(RING_PIECES):
            share_copy(piece, z, core).wait_send()
        return carry

    lax.fori_loop(0, shards, drain_shares, 0)
    for piece in range(RING_PIECES):
        for way in range(2):
            for hop in range(1, hops(piece, way) + 1):
                ring_copy(piece, way, hop, False).wait_send()
    for j in order:
        for turn in range(ROUNDS):
            m_copy(lax.rem(my_y + j, y_size), my_y, turn).wait_send()
    for y in range(y_size):
        for j in range(1, X_SIZE):
            for turn in range(ROUNDS):
                f_copy(lax.rem(my_x + j, X_SIZE), my_x, y, turn).wait_send()
    for c in range(chunks):
        for j in range(1, X_SIZE):
            h_copy(c, lax.rem(my_x + j, X_SIZE), my_x).wait_send()
        for j in order:
            s_copy(c, lax.rem(my_y + j, y_size), my_y).wait_send()


def per_device(
    query_rows,
    key_rows,
    value_rows,
    query_tangent,
    key_tangent,
    value_tangent,
    stream,
    stream_tangent,
    norm_gain,
    expert_ids,
    gate_units,
    slot_index,
    weight_in,
    weight_out,
):
    n = lax.axis_size("seq")
    y_size = lax.axis_size("exp") // X_SIZE
    experts = 2 * y_size
    rows, width = stream.shape
    units = weight_out.shape[0]
    capacity = 2 * ((5 * rows + 4 * experts - 1) // (4 * experts))
    total = n * rows
    chunks = width // CHUNK
    depth = 2 * capacity * chunks
    parts = CHUNK // 128
    back_depth = parts * 2 * capacity
    block = y_size * capacity
    back_size = parts * 2 * block
    pair = 2 * HEAD_DIM
    vmem = pl.BlockSpec(memory_space=pltpu.VMEM)
    away = pl.BlockSpec(memory_space=pltpu.HBM)
    dma = pltpu.SemaphoreType.DMA

    def held(*shape):
        return pltpu.VMEM(shape, BF16)

    results = pl.pallas_call(
        functools.partial(block_kernel, n, y_size, capacity),
        out_shape=jax.ShapeDtypeStruct((2 * rows, width), BF16),
        in_specs=[away] * 14,
        out_specs=vmem,
        scratch_shapes=[
            held(8, rows, width),
            pltpu.VMEM((1, width), F32),
            pltpu.VMEM((3, 2, rows), jnp.int32),
            held(n, width, units),
            held(n * units, width),
            held(n, rows, pair),
            held(n, rows, 2 * pair),
            held(total, pair),
            held(total, 2 * pair),
            held(pair, total),
            held(pair, total),
            held(total, pair),
            held(total, pair),
            held(n, rows, pair),
            held(experts * depth, 2 * chunks * rows),
            held(y_size // 2 * depth, y_size // 2 * depth),
            held(2 * chunks * rows, CHUNK),
            held(y_size, 2 * depth, CHUNK),
            held(y_size, 2 * depth, CHUNK),
            held(X_SIZE, y_size, depth, CHUNK),
            pltpu.VMEM((rows, width), F32),
            pltpu.VMEM((rows, width), F32),
            held(2 * X_SIZE * block, width),
            held(2 * X_SIZE * block, n * units),
            held(back_size, back_size),
            held(2 * parts * rows, experts * back_depth),
            held(2 * parts * rows, experts * back_depth),
            held(chunks, X_SIZE, 2 * block, CHUNK),
            held(chunks, X_SIZE, 2 * block, CHUNK),
            held(chunks, y_size, 2 * back_depth, 128),
            held(chunks, y_size, 2 * back_depth, 128),
        ]
        + [dma((14,))]
        + [dma((n,))] * 6
        + [dma((ROUNDS, y_size))] * 2
        + [dma((ROUNDS, X_SIZE, y_size))] * 2
        + [dma((RING_PIECES, 2 * HOPS))] * 2
        + [dma((RING_PIECES, n // 2))] * 2
        + [dma((chunks, X_SIZE))] * 2
        + [dma((chunks, y_size))] * 2,
        compiler_params=pltpu.CompilerParams(
            collective_id=0, has_side_effects=True, vmem_limit_bytes=56 * 1024 * 1024
        ),
        name="moe_block",
    )(
        query_rows,
        key_rows,
        value_rows,
        query_tangent,
        key_tangent,
        value_tangent,
        stream,
        stream_tangent,
        norm_gain.reshape(1, width),
        expert_ids.T,
        gate_units.T,
        slot_index.T,
        weight_in,
        weight_out,
    )
    return results[:rows], results[rows:]


def solution(mesh):
    rows = P(("exp", "seq"), None)
    return jax.shard_map(
        per_device,
        mesh=mesh,
        in_specs=(rows,) * 8 + (P(),) + (rows,) * 3 + (P(None, ("exp", "seq")), rows),
        out_specs=(rows, rows),
        check_vma=False,
    )
```
